256 devices in a mesh: segment: 8 (over z_lo, x), rep: 32 (over y, z_hi, core).
Axes of the slice: x: 4, y: 4, z: 8 (z_hi: 4, z_lo: 2; z = z_hi * 2 + z_lo), core: 2. Of those that a mesh axis runs over, the one named last changes fastest.
Arguments:
- feature_maps: bfloat16 [2048, 7, 7, 1024], P(('segment', 'rep')), may hold values from -6 to 6
- path_lists: int32 [1, 2048, 1], P(None, ('segment', 'rep')), may hold values from 0 to 7; in each aligned block of 8 rows (0 to 7, 8 to 15, ..., all dimensions but the last counted through in order) at most 2 rows name the same one
- point_weight: bfloat16 [1, 8, 1024, 1024], P(None, 'segment'), may hold values from -0.1875 to 0.1875
- depth_kernel: float32 [1, 8, 25, 1024], P(None, 'segment'), may hold values from -1.8 to 1.8
- cotangent: bfloat16 [2048, 7, 7, 1024], P(('segment', 'rep')), may hold values from -6 to 6
Outputs:
- final_maps: bfloat16 [2048, 7, 7, 1024], P(('segment', 'rep'))
- input_grad: bfloat16 [2048, 7, 7, 1024], P(('segment', 'rep'))
- point_grad: float32 [1, 8, 1024, 1024], P(None, 'segment', 'rep')
- depth_grad: float32 [1, 8, 25, 1024], P(None, 'segment')
The draws below stay inside these ranges and needn't reach their ends.
Inputs may be any that keep to these rules, and one draw needn't show every extreme that they name: `path_lists`: in each layer, among the 8 samples of one device no operator is chosen by more than 2 samples.
All inputs are finite; a program needn't handle non-finite values.
Results may differ from the reference program's by a relative error of at most 0.0032.
Values may be sent and summed in bfloat16 or wider, within the bound.
A program may use at most 128 MiB of HBM per device.

```python
import math
import jax
import jax.numpy as jnp
import numpy as np
from jax import lax

C = 1024
SIDE = 7
SMP_DEV = 8
LAYERS = 1
TAPS = 25
OPS = 8
CAP = 2
SAMPLES = 2048


def steps_of(rng, extent, split, smallest, largest):
    loudness = 1.0
    for dim, blocks in split:
        heights = jax.random.uniform(jax.random.fold_in(jax.random.fold_in(rng, 6), dim), (blocks,), jnp.float32, smallest / len(split), largest / len(split))
        loudness = loudness * jnp.repeat(jnp.exp(heights), extent[dim] // blocks).reshape((-1,) + (1,) * (len(extent) - 1 - dim))
    return loudness


def routed_block(own_key, own, number, rows, number_of, top, limit, skew):
    sequence = jax.random.permutation(own_key, number_of)
    heavy_load, usual = load_shares(number_of, rows * top, limit, skew, True), load_shares(number_of, rows * top, limit, skew, False)
    places = jnp.arange(number_of)

    def named(sizes, offset_by):
        used = int((sizes > 0).sum())
        fixed = max(1, used // 4)
        passed = fixed + (places - fixed + offset_by * (used - fixed)) % max(1, number_of - fixed)
        return jnp.zeros((number_of,), jnp.int32).at[sequence[jnp.where(places < fixed, places, passed)]].set(jnp.asarray(sizes, jnp.int32))

    sizes = jnp.where(number % 4 == 0, named(heavy_load, number // 4), named(usual, number - number // 4 - 1))
    mixed = jax.random.permutation(jax.random.fold_in(own, 3), number_of)
    source_of, taker = mixed[0:number_of // 2 * 2:2], mixed[1:number_of // 2 * 2:2]
    room = jnp.minimum(sizes[source_of] - 1, limit - sizes[taker]) // 2
    room = jnp.where((source_of == sequence[0]) | (taker == sequence[0]) | (sizes[taker] == 0), 0, jnp.maximum(room, 0))
    passed = jax.random.randint(jax.random.fold_in(own, 4), (number_of // 2,), 0, 1 << 20) % (room + 1)
    sizes = sizes.at[source_of].add(-passed).at[taker].add(passed)
    labels = jnp.searchsorted(jnp.cumsum(sizes), jnp.arange(rows * top), side="right").astype(jnp.int32)
    listing = labels.reshape(top, rows).T
    listing = listing[jax.random.permutation(jax.random.fold_in(own, 1), rows)]
    offset_by = jax.random.randint(jax.random.fold_in(own, 2), (rows, 1), 0, top)
    return jnp.take_along_axis(listing, (jnp.arange(top)[None, :] + offset_by) % top, axis=1)


def load_shares(count, total, most, slope, full):
    portions = [(1 << 20) // math.isqrt(rank ** slope) + 1 for rank in range(1, count + 1)]
    largest = most if full else min(most, max(-(-total // count), total * portions[0] // sum(portions)))
    least = 1 if total - largest >= count - 1 else 0
    holding, surplus = [largest] + [least] * (count - 1), total - largest - least * (count - 1)
    while surplus > 0:
        free = [i for i in range(1, count) if holding[i] < largest] or [i for i in range(1, count) if holding[i] < most]
        pool, left = sum([portions[i] for i in free]), surplus
        for i in free:
            extra = min(most - holding[i], max(1, left * portions[i] // pool), surplus)
            holding[i] = holding[i] + extra
            surplus = surplus - extra
    return np.array(holding)


def centred(stream_key, extent, width, reach, shards=(), kind=jnp.bfloat16):
    loudness = steps_of(stream_key, extent, shards, -0.22, 0.18) if shards else 1.0
    drawn = jax.random.normal(stream_key, extent, jnp.float32) * width * loudness
    return jnp.minimum(jnp.maximum(drawn, -reach), reach).astype(kind)


def setup_inputs(seed: int = 0) -> dict:
    key_list = jax.random.split(jax.random.key(seed), 6)
    feature_maps = centred(key_list[0], (SAMPLES, SIDE, SIDE, C), 1.0, 6.0, ((0, 256),))
    path_lists_keys = jax.random.split(jax.random.fold_in(key_list[1], 1), LAYERS * SAMPLES // SMP_DEV)
    path_lists_turns = jax.random.permutation(jax.random.fold_in(key_list[1], 3), LAYERS * SAMPLES // SMP_DEV)
    path_lists = jax.vmap(lambda own, number: routed_block(jax.random.fold_in(key_list[1], 2), own, number, SMP_DEV, OPS, 1, CAP, 2))(path_lists_keys, path_lists_turns).reshape((LAYERS, SAMPLES, 1))
    point_weight = centred(key_list[2], (LAYERS, OPS, C, C), C ** -0.5, 0.1875, ((1, 8),))
    depth_kernel = centred(key_list[3], (LAYERS, OPS, TAPS, C), 0.3, 1.8, ((1, 8),), jnp.float32)
    cotangent = centred(key_list[4], (SAMPLES, SIDE, SIDE, C), 1.0, 6.0, ((0, 256),))
    return dict(feature_maps=feature_maps, path_lists=path_lists, point_weight=point_weight, depth_kernel=depth_kernel, cotangent=cotangent)


EPS = 1e-05

def tap_mask(op_kind):
    tap_index = jnp.arange(25, dtype=jnp.int32)
    row_shift = tap_index // 5 - 2
    col_shift = tap_index % 5 - 2
    narrow = (jnp.abs(row_shift) <= 1) & (jnp.abs(col_shift) <= 1)
    spaced = (row_shift % 2 == 0) & (col_shift % 2 == 0)
    tap_keep = jnp.where(op_kind == 0, narrow, jnp.where(op_kind == 1, True, spaced))
    return tap_keep.astype(jnp.float32)

def shift_window(padded, row_shift, col_shift, map_side):
    return padded[:, 2 + row_shift:2 + row_shift + map_side, 2 + col_shift:2 + col_shift + map_side, :]

def depthwise(source, kernel):
    map_side = source.shape[1]
    padded = jnp.pad(source, ((0, 0), (2, 2), (2, 2), (0, 0)))
    summed = jnp.zeros_like(source)
    for offset in range(25):
        summed = summed + kernel[offset] * shift_window(padded, offset // 5 - 2, offset % 5 - 2, map_side)
    return summed

def depthwise_back(grad_maps, kernel):
    map_side = grad_maps.shape[1]
    padded = jnp.pad(grad_maps, ((0, 0), (2, 2), (2, 2), (0, 0)))
    summed = jnp.zeros_like(grad_maps)
    for offset in range(25):
        summed = summed + kernel[offset] * shift_window(padded, 2 - offset // 5, 2 - offset % 5, map_side)
    return summed

def kernel_grad(grad_maps, source):
    map_side = source.shape[1]
    padded = jnp.pad(source, ((0, 0), (2, 2), (2, 2), (0, 0)))
    tap_rows = [lax.optimization_barrier(jnp.sum(grad_maps * shift_window(padded, offset // 5 - 2, offset % 5 - 2, map_side), axis=(0, 1, 2))) for offset in range(25)]
    return jnp.stack(tap_rows)

def block_forward(inputs, pointwise, kernel):
    channels = inputs.shape[-1]
    source = inputs.astype(jnp.float32)
    mixed_taps = depthwise(source, kernel)
    scaled = mixed_taps * lax.rsqrt(lax.optimization_barrier(jnp.mean(mixed_taps * mixed_taps, axis=-1, keepdims=True)) + EPS)
    active = (scaled * jax.nn.sigmoid(scaled)).astype(jnp.bfloat16)
    branch = jnp.dot(active.reshape(-1, channels), pointwise, preferred_element_type=jnp.float32)
    return (source + branch.reshape(source.shape)).astype(jnp.bfloat16)

def block_backward(inputs, grad_maps, pointwise, kernel):
    channels = inputs.shape[-1]
    source = inputs.astype(jnp.float32)
    mixed_taps = depthwise(source, kernel)
    inverse = lax.rsqrt(lax.optimization_barrier(jnp.mean(mixed_taps * mixed_taps, axis=-1, keepdims=True)) + EPS)
    scaled = mixed_taps * inverse
    logistic = jax.nn.sigmoid(scaled)
    active = (scaled * logistic).astype(jnp.bfloat16)
    flat_grads = grad_maps.reshape(-1, channels)
    back_act = lax.dot_general(flat_grads, pointwise, (((1,), (1,)), ((), ())), preferred_element_type=jnp.float32).reshape(source.shape)
    grad_scaled = back_act * logistic * (1.0 + scaled * (1.0 - logistic))
    grad_mixed = inverse * (grad_scaled - scaled * lax.optimization_barrier(jnp.mean(grad_scaled * scaled, axis=-1, keepdims=True)))
    grad_in = (grad_maps.astype(jnp.float32) + depthwise_back(grad_mixed, kernel)).astype(jnp.bfloat16)
    return (grad_in, active.reshape(-1, channels), flat_grads, kernel_grad(grad_mixed, source))

def point_term(active, flat_grads):
    return lax.dot_general(active, flat_grads, (((0,), (0,)), ((), ())), preferred_element_type=jnp.float32)

def reference(feature_maps, path_lists, point_weight, depth_kernel, cotangent):
    layer_inputs = []
    current = feature_maps
    for layer_at in range(LAYERS):
        layer_inputs.append(current)

        def forward_one(element):
            sample, choose = element
            kernel = depth_kernel[layer_at, choose] * tap_mask(choose % 3)[:, None]
            return block_forward(sample[None], point_weight[layer_at, choose], kernel)[0]
        current = lax.map(forward_one, (current, path_lists[layer_at, :, 0]))
    final_maps = current
    grad_maps = cotangent
    point_list = []
    depth_list = []
    for layer_at in reversed(range(LAYERS)):

        def backward_one(totals, element):
            point_acc, depth_acc = totals
            sample, grad_one, choose = element
            tap_keep = tap_mask(choose % 3)[:, None]
            kernel = depth_kernel[layer_at, choose] * tap_keep
            grad_in, active, flat_grads, depth_term = block_backward(sample[None], grad_one[None], point_weight[layer_at, choose], kernel)
            point_acc = point_acc.at[choose].add(point_term(active, flat_grads))
            depth_acc = depth_acc.at[choose].add(depth_term * tap_keep)
            return ((point_acc, depth_acc), grad_in[0])
        point_init = jnp.zeros(point_weight.shape[1:], jnp.float32)
        depth_init = jnp.zeros(depth_kernel.shape[1:], jnp.float32)
        (point_acc, depth_acc), grad_maps = lax.scan(backward_one, (point_init, depth_init), (layer_inputs[layer_at], grad_maps, path_lists[layer_at, :, 0]))
        point_list.append(point_acc)
        depth_list.append(depth_acc)
    return (final_maps, grad_maps, jnp.stack(point_list[::-1]), jnp.stack(depth_list[::-1]))
```

```python
import functools

import jax
import jax.numpy as jnp
from jax import lax
from jax.experimental import pallas as pl
from jax.experimental.pallas import tpu as pltpu
from jax.sharding import PartitionSpec as P

MESH = pl.DeviceIdType.MESH
EPS = 1e-05
F32 = jnp.float32
BF16 = jnp.bfloat16

C = 1024
SIDE = 7
POS = SIDE * SIDE
MAIN = 48
ROWS = 400
LANES = 128
SEG = 8
PARTNERS = ((1, 0), (0, 1), (0, 3), (1, 1), (1, 3), (0, 2), (1, 2))

XM0, XM1, XL, GM0, GM1, GL, OM0, OM1, OL, IM0, IM1, IL = range(12)


def iota2(rows, cols):
    return (
        lax.broadcasted_iota(jnp.int32, (rows, cols), 0),
        lax.broadcasted_iota(jnp.int32, (rows, cols), 1),
    )


def onehot(cond):
    return jnp.where(cond, 1.0, 0.0)


def mm(a, b):
    return jnp.dot(a, b, preferred_element_type=F32)


def kernel(
    slot_ref,
    x_ref,
    g_ref,
    w_ref,
    k_ref,
    out_ref,
    gin_ref,
    pgrad_ref,
    dgrad_ref,
    sx, rx, sxl, rxl,
    sg, rg, sgl, rgl,
    so, ro, sol, rol,
    si, ri, sil, ril,
    x32, h32, gh32, g32, ab, gb, q128, kb,
    fold_o, fold_i,
    pg, prx, psb, prb, psc, prc,
    dka, dkb, dky, dkz,
    send_sem, recv_sem, local_sem, rsend, rrecv,
):
    me = lax.axis_index("segment")
    rep = lax.axis_index("rep")
    z_lo = me // 4
    xx = me % 4
    my_y = rep // 8
    my_z = (rep // 2) % 4
    core = rep % 2

    def seg_at(dz, dx):
        return ((z_lo + dz) % 2) * 4 + (xx + dx) % 4

    def rep_at(dy, dz, dc):
        return ((my_y + dy) % 4) * 8 + ((my_z + dz) % 4) * 2 + (core + dc) % 2

    rep_partners = ((0, 0, 1), (1, 0, 0), (2, 0, 0), (3, 0, 0), (0, 1, 0), (0, 2, 0), (0, 3, 0))

    barrier = pltpu.get_barrier_semaphore()
    for dz, dx in PARTNERS:
        pl.semaphore_signal(barrier, inc=1, device_id=(seg_at(dz, dx), rep), device_id_type=MESH)
    for dy, dz, dc in rep_partners:
        pl.semaphore_signal(
            barrier, inc=1, device_id=(me, rep_at(dy, dz, dc)), device_id_type=MESH
        )

    def seg_copy(kind, src, dst, there, slot):
        return pltpu.make_async_remote_copy(
            src_ref=src.at[there],
            dst_ref=dst.at[slot],
            send_sem=send_sem.at[kind, there],
            recv_sem=recv_sem.at[kind, slot],
            device_id=(there, rep),
            device_id_type=MESH,
        )

    def seg_send(kind, src, dst):
        for dz, dx in PARTNERS:
            seg_copy(kind, src, dst, seg_at(dz, dx), me).start()
        pltpu.make_async_copy(src.at[me], dst.at[me], local_sem.at[kind]).start()

    def seg_wait(kind, src, dst):
        pltpu.make_async_copy(src.at[me], dst.at[me], local_sem.at[kind]).wait()
        for dz, dx in PARTNERS:
            there = seg_at(dz, dx)
            seg_copy(kind, src, dst, there, there).wait_recv()

    def seg_sent(kind, src, dst):
        for dz, dx in PARTNERS:
            seg_copy(kind, src, dst, seg_at(dz, dx), me).wait_send()

    m, n = iota2(256, 128)
    slots = jnp.broadcast_to(slot_ref[...], (256, 128))
    wanted = 2 * ((m >> 4) & 7) + (m >> 7)
    route32 = onehot(((m & 15) == (n >> 3)) & (slots == wanted))
    route = route32.astype(BF16)
    route_back = route32.T.astype(BF16)
    m, n = iota2(128, 128)
    slots = jnp.broadcast_to(slot_ref[...], (128, 128))
    route_last32 = onehot(((m & 7) == (n >> 3)) & (slots == (m >> 3)))
    route_last = route_last32.astype(BF16)
    route_last_back = route_last32.T.astype(BF16)
    to_rows = onehot(((m >> 3) == (n & 15)) & ((m & 7) == (n >> 4))).astype(BF16)
    from_rows = onehot(((m & 15) == (n >> 3)) & ((m >> 4) == (n & 7))).astype(BF16)
    unfold = onehot(
        ((m >> 4) == (n & 7)) & (((m >> 3) & 1) == ((n >> 3) & 1)) & ((m & 7) == (n >> 4))
    ).astype(BF16)
    refold = onehot(
        ((n >> 4) == (m & 7)) & (((n >> 3) & 1) == ((m >> 3) & 1)) & ((n & 7) == (m >> 4))
    ).astype(BF16)

    def dispatch(source, main, last):
        for q in range(3):
            for part in range(4):
                lanes = slice(part * 256, part * 256 + 256)
                moved = mm(route, source[q * 128 : q * 128 + 128, lanes]).astype(BF16)
                for j in range(2):
                    main[j, :, q * 16 : q * 16 + 16, lanes] = moved[
                        j * 128 : j * 128 + 128
                    ].reshape(8, 16, 256)
        tail = source[384:392, :].astype(F32)
        folded = jnp.concatenate(
            [tail[:, b * LANES : b * LANES + LANES] for b in range(8)]
            + [jnp.zeros((64, LANES), F32)],
            axis=0,
        ).astype(BF16)
        last[...] = mm(route_last, folded).astype(BF16).reshape(8, 16, LANES)

    dispatch(x_ref, sx, sxl)
    pl.semaphore_wait(barrier, 14)
    seg_send(XM0, sx.at[0], rx.at[0])
    seg_send(XL, sxl, rxl)
    dispatch(g_ref, sg, sgl)
    seg_send(GM0, sg.at[0], rg.at[0])
    seg_send(GL, sgl, rgl)
    seg_send(XM1, sx.at[1], rx.at[1])
    seg_send(GM1, sg.at[1], rg.at[1])

    kb[...] = jnp.broadcast_to(k_ref[...][:, None, :], (25, 8, C))
    dka[...] = jnp.zeros((25, 8, C), F32)
    for j in range(2):
        x32[j, 392:400, :] = jnp.zeros((8, C), F32)
        h32[j, 392:400, :] = jnp.zeros((8, C), F32)

    def receive_main(j, got, wide, narrow):
        for q in range(3):
            for part in range(4):
                lanes = slice(part * 256, part * 256 + 256)
                rows = mm(to_rows, got[j, :, q * 16 : q * 16 + 16, lanes].reshape(128, 256))
                wide[j, q * 128 : q * 128 + 128, lanes] = rows
                if narrow is not None:
                    narrow[j, q * 128 : q * 128 + 128, lanes] = rows.astype(BF16)

    def receive_last(got, wide, narrow):
        rows = mm(unfold, got[...].reshape(128, LANES))
        for j in range(2):
            row = jnp.concatenate(
                [rows[b * 16 + j * 8 : b * 16 + j * 8 + 8] for b in range(8)], axis=1
            )
            wide[j, 384:392, :] = row
            if narrow is not None:
                narrow[j, 384:400, :] = jnp.concatenate([row, jnp.zeros((8, C), F32)], 0).astype(BF16)

    def rows_at(ref, j, r, lanes):
        return [ref[j, (r * 7 + c) * 8 : (r * 7 + c) * 8 + 8, lanes] for c in range(7)]

    def convolve(j, source, sign, emit):
        def body(block, carry):
            lanes = pl.ds(pl.multiple_of(block * LANES, LANES), LANES)
            for r in range(7):
                acc = [None] * 7
                for dr in range(-2, 3):
                    at = r + sign * dr
                    if at < 0 or at > 6:
                        continue
                    row = rows_at(source, j, at, lanes)
                    for dc in range(-2, 3):
                        tap = kb[(dr + 2) * 5 + dc + 2, :, lanes]
                        for c in range(7):
                            ac = c + sign * dc
                            if ac < 0 or ac > 6:
                                continue
                            term = tap * row[ac]
                            acc[c] = term if acc[c] is None else acc[c] + term
                for c in range(7):
                    emit(j, (r * 7 + c) * 8, lanes, acc[c])
            return carry

        lax.fori_loop(0, 8, body, 0)

    def emit_h(j, row, lanes, value):
        h32[j, row : row + 8, lanes] = value

    def emit_gin(j, row, lanes, value):
        g32[j, row : row + 8, lanes] = g32[j, row : row + 8, lanes] + value

    def tap_grad(j):
        def body(block, carry):
            lanes = pl.ds(pl.multiple_of(block * LANES, LANES), LANES)
            for dr in range(-2, 3):
                acc = [None] * 5
                for r in range(7):
                    at = r + dr
                    if at < 0 or at > 6:
                        continue
                    grad = rows_at(gh32, j, r, lanes)
                    row = rows_at(x32, j, at, lanes)
                    for dc in range(-2, 3):
                        for c in range(7):
                            ac = c + dc
                            if ac < 0 or ac > 6:
                                continue
                            term = grad[c] * row[ac]
                            acc[dc + 2] = term if acc[dc + 2] is None else acc[dc + 2] + term
                for t in range(5):
                    at = (dr + 2) * 5 + t
                    dka[at, :, lanes] = dka[at, :, lanes] + acc[t]
            return carry

        lax.fori_loop(0, 8, body, 0)

    def activate(j):
        def body(step, carry):
            rows = pl.ds(pl.multiple_of(step * 80, 80), 80)
            h = h32[j, rows, :]
            q = lax.rsqrt(jnp.sum(h * h, axis=1, keepdims=True) * (1.0 / C) + EPS)
            z = h * q
            h32[j, rows, :] = z
            q128[j, rows, :] = jnp.broadcast_to(q, (80, LANES))
            ab[j, rows, :] = (z * jax.nn.sigmoid(z)).astype(BF16)
            return carry

        lax.fori_loop(0, 5, body, 0)

    def send_rows(j, value, n, main, fold):
        lanes = pl.ds(pl.multiple_of(n * 256, 256), 256)
        for q in range(3):
            moved = mm(from_rows, value[q * 128 : q * 128 + 128]).astype(BF16)
            main[j, :, q * 16 : q * 16 + 16, lanes] = moved.reshape(8, 16, 256)
        tail = value[384:400].astype(F32)
        for b in range(2):
            fold[pl.ds(pl.multiple_of((2 * n + b) * 16 + j * 8, 8), 8), :] = tail[
                :8, b * LANES : b * LANES + LANES
            ]

    def send_last(fold, last):
        last[...] = mm(refold, fold[...].astype(BF16)).astype(BF16).reshape(8, 16, LANES)

    def project(j):
        def body(n, carry):
            lanes = pl.ds(pl.multiple_of(n * 256, 256), 256)
            value = (x32[j, :, lanes] + mm(ab[j], w_ref[:, lanes])).astype(BF16)
            send_rows(j, value, n, so, fold_o)
            return carry

        lax.fori_loop(0, 4, body, 0)

    def back_project(j):
        def body(n, carry):
            lanes = pl.ds(pl.multiple_of(n * 256, 256), 256)
            gh32[j, :, lanes] = lax.dot_general(
                gb[j], w_ref[lanes, :], (((1,), (1,)), ((), ())), preferred_element_type=F32
            )
            return carry

        lax.fori_loop(0, 4, body, 0)

    def back_activate(j):
        def body(step, carry):
            rows = pl.ds(pl.multiple_of(step * 80, 80), 80)
            z = h32[j, rows, :]
            s = jax.nn.sigmoid(z)
            gz = gh32[j, rows, :] * s * (1.0 + z * (1.0 - s))
            mean = jnp.sum(gz * z, axis=1, keepdims=True) * (1.0 / C)
            q = jnp.concatenate([q128[j, rows, :]] * 8, axis=1)
            gh32[j, rows, :] = q * (gz - z * mean)
            return carry

        lax.fori_loop(0, 5, body, 0)

    def send_gin(j):
        def body(n, carry):
            lanes = pl.ds(pl.multiple_of(n * 256, 256), 256)
            send_rows(j, g32[j, :, lanes].astype(BF16), n, si, fold_i)
            return carry

        lax.fori_loop(0, 4, body, 0)

    def forward(j):
        seg_wait((XM0, XM1)[j], sx.at[j], rx.at[j])
        receive_main(j, rx, x32, None)
        if j == 0:
            seg_wait(XL, sxl, rxl)
            receive_last(rxl, x32, None)
        convolve(j, x32, 1, emit_h)
        activate(j)
        project(j)
        seg_send((OM0, OM1)[j], so.at[j], ro.at[j])
        if j == 1:
            send_last(fold_o, sol)
            seg_send(OL, sol, rol)

    def receive_g(j):
        seg_wait((GM0, GM1)[j], sg.at[j], rg.at[j])
        receive_main(j, rg, g32, gb)
        if j == 0:
            seg_wait(GL, sgl, rgl)
            receive_last(rgl, g32, gb)
            for i in range(2):
                g32[i, 392:400, :] = jnp.zeros((8, C), F32)

    def backward(j):
        back_project(j)
        back_activate(j)
        convolve(j, gh32, -1, emit_gin)
        send_gin(j)
        seg_send((IM0, IM1)[j], si.at[j], ri.at[j])

    def home(main, last, target):
        for q in range(3):
            for part in range(4):
                lanes = slice(part * 256, part * 256 + 256)
                got = jnp.concatenate(
                    [main[j, :, q * 16 : q * 16 + 16, lanes].reshape(128, 256) for j in range(2)],
                    axis=0,
                )
                target[q * 128 : q * 128 + 128, lanes] = mm(route_back, got).astype(BF16)
        rows = mm(route_last_back, last[...].reshape(128, LANES))
        target[384:392, :] = jnp.concatenate(
            [rows[b * 8 : b * 8 + 8] for b in range(8)], axis=1
        ).astype(BF16)

    def rep_copy(kind, src, dst, dy, dz, dc):
        return pltpu.make_async_remote_copy(
            src_ref=src,
            dst_ref=dst,
            send_sem=rsend.at[kind],
            recv_sem=rrecv.at[kind],
            device_id=(me, rep_at(dy, dz, dc)),
            device_id_type=MESH,
        )

    sibling = (core + 1) % 2

    def pair_copy(y):
        return rep_copy(y, pg.at[y, :, sibling], prx.at[y], 0, 0, 1)

    def point_terms():
        for y in range(4):
            cols = slice(y * 256, y * 256 + 256)
            for part in range(4):
                lanes = slice(part * 256, part * 256 + 256)
                total = None
                for j in range(2):
                    term = lax.dot_general(
                        ab[j, :, cols],
                        gb[j, :, lanes],
                        (((0,), (0,)), ((), ())),
                        preferred_element_type=F32,
                    )
                    total = term if total is None else total + term
                pg[y, :, :, :, lanes] = total.reshape(4, 2, 32, 256)
            pair_copy(y).start()

    def y_copy(dy):
        return rep_copy(3 + dy, psb.at[dy - 1], prb.at[dy - 1], dy, 0, 0)

    def z_copy(dz):
        return rep_copy(6 + dz, psc.at[dz - 1], prc.at[dz - 1], 0, dz, 0)

    def point_over_y():
        for dy in (1, 2, 3, 0):
            y = (my_y + dy) % 4
            pair_copy(y).wait_recv()
            total = pg[y, :, core] + prx[y]
            if dy:
                psb[dy - 1] = total.astype(BF16)
                y_copy(dy).start()
            else:
                prx[y] = total

    def point_over_z():
        total = prx[my_y]
        for dy in (1, 2, 3):
            y_copy(dy).wait_recv()
        for slot in range(3):
            total = total + prb[slot].astype(F32)
        prx[my_y] = total
        for dz in (1, 2, 3):
            psc[dz - 1] = prx[my_y, (my_z + dz) % 4].astype(BF16)
            z_copy(dz).start()

    def point_end():
        for dz in (1, 2, 3):
            z_copy(dz).wait_recv()
        total = prx[my_y, my_z]
        for slot in range(3):
            total = total + prc[slot].astype(F32)
        pgrad_ref[...] = total

    def tap_pair():
        return rep_copy(10, dkb.at[0], dkb.at[1], 0, 0, 1)

    def tap_y(dy, slot):
        return rep_copy(10 + dy, dky.at[my_y], dky.at[slot], dy, 0, 0)

    def tap_z(dz, slot):
        return rep_copy(13 + dz, dkz.at[my_z], dkz.at[slot], 0, dz, 0)

    forward(0)
    receive_g(0)
    backward(0)
    forward(1)
    receive_g(1)
    point_terms()
    back_project(1)
    back_activate(1)
    point_over_y()
    tap_grad(0)
    tap_grad(1)
    dkb[0] = jnp.concatenate([jnp.sum(dka[...], axis=1), jnp.zeros((7, C), F32)], axis=0)
    tap_pair().start()
    convolve(1, gh32, -1, emit_gin)
    send_gin(1)
    seg_send(IM1, si.at[1], ri.at[1])
    send_last(fold_i, sil)
    seg_send(IL, sil, ril)
    point_over_z()
    tap_pair().wait_recv()
    dky[my_y] = dkb[0] + dkb[1]
    for dy in (1, 2, 3):
        tap_y(dy, my_y).start()

    seg_wait(OM0, so.at[0], ro.at[0])
    seg_wait(OM1, so.at[1], ro.at[1])
    seg_wait(OL, sol, rol)
    home(ro, rol, out_ref)
    for dy in (1, 2, 3):
        tap_y(dy, (my_y + 4 - dy) % 4).wait_recv()
    dkz[my_z] = (dky[0] + dky[1]) + (dky[2] + dky[3])
    for dz in (1, 2, 3):
        tap_z(dz, my_z).start()
    point_end()
    seg_wait(IM0, si.at[0], ri.at[0])
    seg_wait(IM1, si.at[1], ri.at[1])
    seg_wait(IL, sil, ril)
    home(ri, ril, gin_ref)
    for dz in (1, 2, 3):
        tap_z(dz, (my_z + 4 - dz) % 4).wait_recv()
    dgrad_ref[...] = ((dkz[0] + dkz[1]) + (dkz[2] + dkz[3]))[:25]

    for j in range(2):
        seg_sent((XM0, XM1)[j], sx.at[j], rx.at[j])
        seg_sent((GM0, GM1)[j], sg.at[j], rg.at[j])
        seg_sent((OM0, OM1)[j], so.at[j], ro.at[j])
        seg_sent((IM0, IM1)[j], si.at[j], ri.at[j])
    seg_sent(XL, sxl, rxl)
    seg_sent(GL, sgl, rgl)
    seg_sent(OL, sol, rol)
    seg_sent(IL, sil, ril)
    for y in range(4):
        pair_copy(y).wait_send()
    tap_pair().wait_send()
    for d in (1, 2, 3):
        y_copy(d).wait_send()
        z_copy(d).wait_send()
        tap_y(d, my_y).wait_send()
        tap_z(d, my_z).wait_send()


def tap_mask(op_kind):
    tap_index = jnp.arange(25, dtype=jnp.int32)
    row_shift = tap_index // 5 - 2
    col_shift = tap_index % 5 - 2
    narrow = (jnp.abs(row_shift) <= 1) & (jnp.abs(col_shift) <= 1)
    spaced = (row_shift % 2 == 0) & (col_shift % 2 == 0)
    tap_keep = jnp.where(op_kind == 0, narrow, jnp.where(op_kind == 1, True, spaced))
    return tap_keep.astype(jnp.float32)


def body(feature_maps, path_lists, point_weight, depth_kernel, cotangent):
    section = lax.axis_index("segment")
    path = path_lists[0, :, 0]
    index = jnp.arange(8, dtype=jnp.int32)
    same = (path[None, :] == path[:, None]) & (index[None, :] < index[:, None])
    slot = path * 2 + jnp.sum(same.astype(jnp.int32), axis=1)
    slots = jnp.tile(slot, 16)[None, :]
    keep = tap_mask(section % 3)[:, None]
    x = feature_maps.transpose(1, 2, 0, 3).reshape(POS * 8, C)
    g = cotangent.transpose(1, 2, 0, 3).reshape(POS * 8, C)
    vmem = pl.BlockSpec(memory_space=pltpu.VMEM)
    main = pltpu.VMEM((2, SEG, MAIN, C), BF16)
    last = pltpu.VMEM((SEG, 16, LANES), BF16)
    wide = pltpu.VMEM((2, ROWS, C), F32)
    narrow = pltpu.VMEM((2, ROWS, C), BF16)
    out, gin, pgrad, dgrad = pl.pallas_call(
        kernel,
        out_shape=(
            jax.ShapeDtypeStruct((POS * 8, C), BF16),
            jax.ShapeDtypeStruct((POS * 8, C), BF16),
            jax.ShapeDtypeStruct((32, C), F32),
            jax.ShapeDtypeStruct((25, C), F32),
        ),
        in_specs=[vmem] * 5,
        out_specs=[vmem] * 4,
        scratch_shapes=[
            *[main, main, last, last] * 4,
            wide, wide, wide, wide, narrow, narrow,
            pltpu.VMEM((2, ROWS, LANES), F32),
            pltpu.VMEM((25, 8, C), F32),
            pltpu.VMEM((128, LANES), F32),
            pltpu.VMEM((128, LANES), F32),
            pltpu.VMEM((4, 4, 2, 32, C), F32),
            pltpu.VMEM((4, 4, 32, C), F32),
            pltpu.VMEM((3, 4, 32, C), BF16),
            pltpu.VMEM((3, 4, 32, C), BF16),
            pltpu.VMEM((3, 32, C), BF16),
            pltpu.VMEM((3, 32, C), BF16),
            pltpu.VMEM((25, 8, C), F32),
            pltpu.VMEM((2, 32, C), F32),
            pltpu.VMEM((4, 32, C), F32),
            pltpu.VMEM((4, 32, C), F32),
            pltpu.SemaphoreType.DMA((12, SEG)),
            pltpu.SemaphoreType.DMA((12, SEG)),
            pltpu.SemaphoreType.DMA((12,)),
            pltpu.SemaphoreType.DMA((17,)),
            pltpu.SemaphoreType.DMA((17,)),
        ],
        compiler_params=pltpu.CompilerParams(
            collective_id=0, has_side_effects=True, vmem_limit_bytes=60 * 1024 * 1024
        ),
        name="supernet_window",
    )(slots, x, g, point_weight[0, 0], depth_kernel[0, 0] * keep)
    final = out.reshape(SIDE, SIDE, 8, C).transpose(2, 0, 1, 3)
    grad = gin.reshape(SIDE, SIDE, 8, C).transpose(2, 0, 1, 3)
    return final, grad, pgrad[None, None], (dgrad * keep)[None, None]


def solution(mesh):
    placed = (
        P(("segment", "rep"), None, None, None),
        P(None, ("segment", "rep"), None),
        P(None, "segment", None, None),
        P(None, "segment", None, None),
        P(("segment", "rep"), None, None, None),
    )
    return jax.shard_map(
        body,
        mesh=mesh,
        in_specs=placed,
        out_specs=(
            P(("segment", "rep"), None, None, None),
            P(("segment", "rep"), None, None, None),
            P(None, "segment", "rep", None),
            P(None, "segment", None, None),
        ),
        check_vma=False,
    )
```

```python
import functools

import jax
import jax.numpy as jnp
from jax import lax
from jax.experimental import pallas as pl
from jax.experimental.pallas import tpu as pltpu
from jax.sharding import PartitionSpec as P

MESH = pl.DeviceIdType.MESH
EPS = 1e-05
F32 = jnp.float32
BF16 = jnp.bfloat16

C = 1024
SIDE = 7
POS = SIDE * SIDE
MAIN = 48
ROWS = 400
LANES = 128
SEG = 8
PARTNERS = ((1, 0), (0, 1), (0, 3), (1, 1), (1, 3), (0, 2), (1, 2))

XM0, XM1, XL, GM0, GM1, GL, OM0, OM1, OL, IM0, IM1, IL = range(12)


def iota2(rows, cols):
    return (
        lax.broadcasted_iota(jnp.int32, (rows, cols), 0),
        lax.broadcasted_iota(jnp.int32, (rows, cols), 1),
    )


def onehot(cond):
    return jnp.where(cond, 1.0, 0.0)


def mm(a, b):
    return jnp.dot(a, b, preferred_element_type=F32)


def kernel(
    path_ref,
    x_ref,
    g_ref,
    w_ref,
    k_ref,
    out_ref,
    gin_ref,
    pgrad_ref,
    dgrad_ref,
    sx, rx, sxl, rxl,
    sg, rg, sgl, rgl,
    so, ro, sol, rol,
    si, ri, sil, ril,
    x32, h32, gh32, g32, ab, gb, q128, kb,
    fold_o, fold_i,
    pg, prx, psb, prb, psc, prc,
    dka, tap_own, tap_pair_in, tap_y_in, tap_z_all, tap_all,
    send_sem, recv_sem, local_sem, rsend, rrecv,
):
    me = lax.axis_index("segment")
    rep = lax.axis_index("rep")
    z_lo = me // 4
    xx = me % 4
    my_y = rep // 8
    my_z = (rep // 2) % 4
    core = rep % 2

    def seg_at(dz, dx):
        return ((z_lo + dz) % 2) * 4 + (xx + dx) % 4

    def rep_at(dy, dz, dc):
        return ((my_y + dy) % 4) * 8 + ((my_z + dz) % 4) * 2 + (core + dc) % 2

    rep_partners = ((0, 0, 1), (1, 0, 0), (2, 0, 0), (3, 0, 0), (0, 1, 0), (0, 2, 0), (0, 3, 0))

    barrier = pltpu.get_barrier_semaphore()
    for dz, dx in PARTNERS:
        pl.semaphore_signal(barrier, inc=1, device_id=(seg_at(dz, dx), rep), device_id_type=MESH)
    for dy, dz, dc in rep_partners:
        pl.semaphore_signal(
            barrier, inc=1, device_id=(me, rep_at(dy, dz, dc)), device_id_type=MESH
        )

    def seg_copy(kind, src, dst, there, slot):
        return pltpu.make_async_remote_copy(
            src_ref=src.at[there],
            dst_ref=dst.at[slot],
            send_sem=send_sem.at[kind, there],
            recv_sem=recv_sem.at[kind, slot],
            device_id=(there, rep),
            device_id_type=MESH,
        )

    def seg_send(kind, src, dst):
        for dz, dx in PARTNERS:
            seg_copy(kind, src, dst, seg_at(dz, dx), me).start()
        pltpu.make_async_copy(src.at[me], dst.at[me], local_sem.at[kind]).start()

    def seg_wait(kind, src, dst):
        pltpu.make_async_copy(src.at[me], dst.at[me], local_sem.at[kind]).wait()
        for dz, dx in PARTNERS:
            there = seg_at(dz, dx)
            seg_copy(kind, src, dst, there, there).wait_recv()

    def seg_sent(kind, src, dst):
        for dz, dx in PARTNERS:
            seg_copy(kind, src, dst, seg_at(dz, dx), me).wait_send()

    paths = [path_ref[0, i] for i in range(8)]
    slot_of = []
    for i in range(8):
        rank = jnp.int32(0)
        for earlier in range(i):
            rank = rank + jnp.where(paths[earlier] == paths[i], 1, 0)
        slot_of.append(2 * paths[i] + rank)

    def slots_like(sample):
        slots = jnp.full(sample.shape, -1, jnp.int32)
        for i in range(8):
            slots = jnp.where(sample == i, slot_of[i], slots)
        return slots

    m, n = iota2(256, 128)
    slots = slots_like(n & 7)
    wanted = 2 * ((m >> 4) & 7) + (m >> 7)
    route32 = onehot(((m & 15) == (n >> 3)) & (slots == wanted))
    route = route32.astype(BF16)
    route_back = route32.T.astype(BF16)
    m, n = iota2(128, 128)
    slots = slots_like(n & 7)
    route_last32 = onehot(((m & 7) == (n >> 3)) & (slots == (m >> 3)))
    route_last = route_last32.astype(BF16)
    route_last_back = route_last32.T.astype(BF16)
    to_rows = onehot(((m >> 3) == (n & 15)) & ((m & 7) == (n >> 4))).astype(BF16)
    from_rows = onehot(((m & 15) == (n >> 3)) & ((m >> 4) == (n & 7))).astype(BF16)
    unfold = onehot(
        ((m >> 4) == (n & 7)) & (((m >> 3) & 1) == ((n >> 3) & 1)) & ((m & 7) == (n >> 4))
    ).astype(BF16)
    refold = onehot(
        ((n >> 4) == (m & 7)) & (((n >> 3) & 1) == ((m >> 3) & 1)) & ((n & 7) == (m >> 4))
    ).astype(BF16)

    def dispatch(source, main, last):
        for q in range(3):
            for part in range(4):
                lanes = slice(part * 256, part * 256 + 256)
                moved = mm(route, source[q * 128 : q * 128 + 128, lanes]).astype(BF16)
                for j in range(2):
                    main[j, :, q * 16 : q * 16 + 16, lanes] = moved[
                        j * 128 : j * 128 + 128
                    ].reshape(8, 16, 256)
        tail = source[384:392, :].astype(F32)
        folded = jnp.concatenate(
            [tail[:, b * LANES : b * LANES + LANES] for b in range(8)]
            + [jnp.zeros((64, LANES), F32)],
            axis=0,
        ).astype(BF16)
        last[...] = mm(route_last, folded).astype(BF16).reshape(8, 16, LANES)

    dispatch(x_ref, sx, sxl)
    pl.semaphore_wait(barrier, 14)
    seg_send(XM0, sx.at[0], rx.at[0])
    seg_send(XL, sxl, rxl)
    dispatch(g_ref, sg, sgl)
    seg_send(GM0, sg.at[0], rg.at[0])
    seg_send(GL, sgl, rgl)
    seg_send(XM1, sx.at[1], rx.at[1])
    seg_send(GM1, sg.at[1], rg.at[1])

    kind = me % 3
    keep = []
    for t in range(25):
        row, col = t // 5 - 2, t % 5 - 2
        narrow = 1.0 if abs(row) <= 1 and abs(col) <= 1 else 0.0
        spaced = 1.0 if row % 2 == 0 and col % 2 == 0 else 0.0
        keep.append(jnp.where(kind == 0, narrow, jnp.where(kind == 1, 1.0, spaced)))
        kb[t] = jnp.broadcast_to(k_ref[t], (8, C)) * keep[t]
    dka[...] = jnp.zeros((25, 8, C), F32)
    for j in range(2):
        x32[j, 392:400, :] = jnp.zeros((8, C), F32)
        h32[j, 392:400, :] = jnp.zeros((8, C), F32)

    def receive_main(j, got, wide, narrow):
        for q in range(3):
            for part in range(4):
                lanes = slice(part * 256, part * 256 + 256)
                rows = mm(to_rows, got[j, :, q * 16 : q * 16 + 16, lanes].reshape(128, 256))
                wide[j, q * 128 : q * 128 + 128, lanes] = rows
                if narrow is not None:
                    narrow[j, q * 128 : q * 128 + 128, lanes] = rows.astype(BF16)

    def receive_last(got, wide, narrow):
        rows = mm(unfold, got[...].reshape(128, LANES))
        for j in range(2):
            row = jnp.concatenate(
                [rows[b * 16 + j * 8 : b * 16 + j * 8 + 8] for b in range(8)], axis=1
            )
            wide[j, 384:392, :] = row
            if narrow is not None:
                narrow[j, 384:400, :] = jnp.concatenate([row, jnp.zeros((8, C), F32)], 0).astype(BF16)

    def rows_at(ref, j, r, lanes):
        return [ref[j, (r * 7 + c) * 8 : (r * 7 + c) * 8 + 8, lanes] for c in range(7)]

    def convolve(j, source, sign, emit):
        def body(block, carry):
            lanes = pl.ds(pl.multiple_of(block * LANES, LANES), LANES)
            for r in range(7):
                acc = [None] * 7
                for dr in range(-2, 3):
                    at = r + sign * dr
                    if at < 0 or at > 6:
                        continue
                    row = rows_at(source, j, at, lanes)
                    for dc in range(-2, 3):
                        tap = kb[(dr + 2) * 5 + dc + 2, :, lanes]
                        for c in range(7):
                            ac = c + sign * dc
                            if ac < 0 or ac > 6:
                                continue
                            term = tap * row[ac]
                            acc[c] = term if acc[c] is None else acc[c] + term
                for c in range(7):
                    emit(j, (r * 7 + c) * 8, lanes, acc[c])
            return carry

        lax.fori_loop(0, 8, body, 0)

    def emit_h(j, row, lanes, value):
        h32[j, row : row + 8, lanes] = value

    def emit_gin(j, row, lanes, value):
        g32[j, row : row + 8, lanes] = g32[j, row : row + 8, lanes] + value

    def tap_grad(j):
        def body(block, carry):
            lanes = pl.ds(pl.multiple_of(block * LANES, LANES), LANES)
            for dr in range(-2, 3):
                acc = [None] * 5
                for r in range(7):
                    at = r + dr
                    if at < 0 or at > 6:
                        continue
                    grad = rows_at(gh32, j, r, lanes)
                    row = rows_at(x32, j, at, lanes)
                    for dc in range(-2, 3):
                        for c in range(7):
                            ac = c + dc
                            if ac < 0 or ac > 6:
                                continue
                            term = grad[c] * row[ac]
                            acc[dc + 2] = term if acc[dc + 2] is None else acc[dc + 2] + term
                for t in range(5):
                    at = (dr + 2) * 5 + t
                    dka[at, :, lanes] = dka[at, :, lanes] + acc[t]
            return carry

        lax.fori_loop(0, 8, body, 0)

    def activate(j):
        def body(step, carry):
            rows = pl.ds(pl.multiple_of(step * 80, 80), 80)
            h = h32[j, rows, :]
            q = lax.rsqrt(jnp.sum(h * h, axis=1, keepdims=True) * (1.0 / C) + EPS)
            z = h * q
            h32[j, rows, :] = z
            q128[j, rows, :] = jnp.broadcast_to(q, (80, LANES))
            ab[j, rows, :] = (z * jax.nn.sigmoid(z)).astype(BF16)
            return carry

        lax.fori_loop(0, 5, body, 0)

    def send_rows(j, value, n, main, fold):
        lanes = pl.ds(pl.multiple_of(n * 256, 256), 256)
        for q in range(3):
            moved = mm(from_rows, value[q * 128 : q * 128 + 128]).astype(BF16)
            main[j, :, q * 16 : q * 16 + 16, lanes] = moved.reshape(8, 16, 256)
        tail = value[384:400].astype(F32)
        for b in range(2):
            fold[pl.ds(pl.multiple_of((2 * n + b) * 16 + j * 8, 8), 8), :] = tail[
                :8, b * LANES : b * LANES + LANES
            ]

    def send_last(fold, last):
        last[...] = mm(refold, fold[...].astype(BF16)).astype(BF16).reshape(8, 16, LANES)

    def project(j):
        def body(n, carry):
            lanes = pl.ds(pl.multiple_of(n * 256, 256), 256)
            value = (x32[j, :, lanes] + mm(ab[j], w_ref[:, lanes])).astype(BF16)
            send_rows(j, value, n, so, fold_o)
            return carry

        lax.fori_loop(0, 4, body, 0)

    def back_project(j):
        def body(n, carry):
            lanes = pl.ds(pl.multiple_of(n * 256, 256), 256)
            gh32[j, :, lanes] = lax.dot_general(
                gb[j], w_ref[lanes, :], (((1,), (1,)), ((), ())), preferred_element_type=F32
            )
            return carry

        lax.fori_loop(0, 4, body, 0)

    def back_activate(j):
        def body(step, carry):
            rows = pl.ds(pl.multiple_of(step * 80, 80), 80)
            z = h32[j, rows, :]
            s = jax.nn.sigmoid(z)
            gz = gh32[j, rows, :] * s * (1.0 + z * (1.0 - s))
            mean = jnp.sum(gz * z, axis=1, keepdims=True) * (1.0 / C)
            q = jnp.concatenate([q128[j, rows, :]] * 8, axis=1)
            gh32[j, rows, :] = q * (gz - z * mean)
            return carry

        lax.fori_loop(0, 5, body, 0)

    def send_gin(j):
        def body(n, carry):
            lanes = pl.ds(pl.multiple_of(n * 256, 256), 256)
            send_rows(j, g32[j, :, lanes].astype(BF16), n, si, fold_i)
            return carry

        lax.fori_loop(0, 4, body, 0)

    def forward(j):
        seg_wait((XM0, XM1)[j], sx.at[j], rx.at[j])
        receive_main(j, rx, x32, None)
        if j == 0:
            seg_wait(XL, sxl, rxl)
            receive_last(rxl, x32, None)
        convolve(j, x32, 1, emit_h)
        activate(j)
        project(j)
        seg_send((OM0, OM1)[j], so.at[j], ro.at[j])
        if j == 1:
            send_last(fold_o, sol)
            seg_send(OL, sol, rol)

    def receive_g(j):
        seg_wait((GM0, GM1)[j], sg.at[j], rg.at[j])
        receive_main(j, rg, g32, gb)
        if j == 0:
            seg_wait(GL, sgl, rgl)
            receive_last(rgl, g32, gb)
            for i in range(2):
                g32[i, 392:400, :] = jnp.zeros((8, C), F32)

    def backward(j):
        back_project(j)
        back_activate(j)
        convolve(j, gh32, -1, emit_gin)
        send_gin(j)
        seg_send((IM0, IM1)[j], si.at[j], ri.at[j])

    def home(main, last, target):
        for q in range(3):
            for part in range(4):
                lanes = slice(part * 256, part * 256 + 256)
                got = jnp.concatenate(
                    [main[j, :, q * 16 : q * 16 + 16, lanes].reshape(128, 256) for j in range(2)],
                    axis=0,
                )
                target[q * 128 : q * 128 + 128, lanes] = mm(route_back, got).astype(BF16)
        rows = mm(route_last_back, last[...].reshape(128, LANES))
        target[384:392, :] = jnp.concatenate(
            [rows[b * 8 : b * 8 + 8] for b in range(8)], axis=1
        ).astype(BF16)

    def rep_copy(kind, src, dst, dy, dz, dc):
        return pltpu.make_async_remote_copy(
            src_ref=src,
            dst_ref=dst,
            send_sem=rsend.at[kind],
            recv_sem=rrecv.at[kind],
            device_id=(me, rep_at(dy, dz, dc)),
            device_id_type=MESH,
        )

    sibling = (core + 1) % 2

    def pair_copy(y):
        return rep_copy(y, pg.at[y, :, sibling], prx.at[y], 0, 0, 1)

    def point_terms(j):
        for dy in (1, 2, 3, 0):
            y = (my_y + dy) % 4
            cols = pl.ds(pl.multiple_of(y * 256, 256), 256)
            for part in range(4):
                lanes = slice(part * 256, part * 256 + 256)
                term = lax.dot_general(
                    ab[j, :, cols],
                    gb[j, :, lanes],
                    (((0,), (0,)), ((), ())),
                    preferred_element_type=F32,
                ).reshape(4, 2, 32, 256)
                if j == 0:
                    pg[y, :, :, :, lanes] = term
                else:
                    pg[y, :, :, :, lanes] = pg[y, :, :, :, lanes] + term
            if j == 1:
                pair_copy(y).start()

    def y_copy(dy):
        return rep_copy(3 + dy, psb.at[dy - 1], prb.at[dy - 1], dy, 0, 0)

    def z_copy(dz):
        return rep_copy(6 + dz, psc.at[dz - 1], prc.at[dz - 1], 0, dz, 0)

    def point_over_y():
        for dy in (1, 2, 3, 0):
            y = (my_y + dy) % 4
            pair_copy(y).wait_recv()
            total = pg[y, :, core] + prx[y]
            if dy:
                psb[dy - 1] = total.astype(BF16)
                y_copy(dy).start()
            else:
                prx[y] = total

    def point_over_z():
        total = prx[my_y]
        for dy in (1, 2, 3):
            y_copy(dy).wait_recv()
        for slot in range(3):
            total = total + prb[slot].astype(F32)
        prx[my_y] = total
        for dz in (1, 2, 3):
            psc[dz - 1] = prx[my_y, (my_z + dz) % 4].astype(BF16)
            z_copy(dz).start()

    def point_end():
        for dz in (1, 2, 3):
            z_copy(dz).wait_recv()
        total = prx[my_y, my_z]
        for slot in range(3):
            total = total + prc[slot].astype(F32)
        pgrad_ref[...] = total

    def tap_pair():
        return rep_copy(10, tap_own.at[sibling], tap_pair_in, 0, 0, 1)

    def tap_y(dy):
        return rep_copy(10 + dy, tap_own.at[core, (my_y + dy) % 4], tap_y_in.at[dy - 1], dy, 0, 0)

    def tap_z(dz, slot):
        return rep_copy(13 + dz, tap_z_all.at[my_z], tap_z_all.at[slot], 0, dz, 0)

    def tap_back_y(dy, slot):
        return rep_copy(16 + dy, tap_all.at[core, my_y], tap_all.at[core, slot], dy, 0, 0)

    def tap_back_pair(slot):
        return rep_copy(20, tap_all.at[core], tap_all.at[slot], 0, 0, 1)

    def taps_to_pair():
        sums = jnp.concatenate([jnp.sum(dka[...], axis=1), jnp.zeros((7, C), F32)], axis=0)
        for block in range(8):
            tap_own[block // 4, block % 4] = sums[:, block * LANES : block * LANES + LANES]
        tap_pair().start()

    def taps_to_y():
        tap_pair().wait_recv()
        tap_own[core] = tap_own[core] + tap_pair_in[...]
        for dy in (1, 2, 3):
            tap_y(dy).start()

    def taps_to_z():
        total = tap_own[core, my_y]
        for dy in (1, 2, 3):
            tap_y(dy).wait_recv()
            total = total + tap_y_in[dy - 1]
        tap_z_all[my_z] = total
        for dz in (1, 2, 3):
            tap_z(dz, my_z).start()

    def taps_back_y():
        for dz in (1, 2, 3):
            tap_z(dz, (my_z + 4 - dz) % 4).wait_recv()
        tap_all[core, my_y] = (tap_z_all[0] + tap_z_all[1]) + (tap_z_all[2] + tap_z_all[3])
        for dy in (1, 2, 3):
            tap_back_y(dy, my_y).start()

    def taps_back_pair():
        for dy in (1, 2, 3):
            tap_back_y(dy, (my_y + 4 - dy) % 4).wait_recv()
        tap_back_pair(core).start()

    def taps_end():
        tap_back_pair(sibling).wait_recv()
        sums = jnp.concatenate([tap_all[b // 4, b % 4] for b in range(8)], axis=1)
        for t in range(25):
            dgrad_ref[t] = sums[t : t + 1] * keep[t]

    forward(0)
    receive_g(0)
    backward(0)
    tap_grad(0)
    point_terms(0)
    forward(1)
    receive_g(1)
    point_terms(1)
    back_project(1)
    back_activate(1)
    point_over_y()
    convolve(1, gh32, -1, emit_gin)
    send_gin(1)
    seg_send(IM1, si.at[1], ri.at[1])
    send_last(fold_i, sil)
    seg_send(IL, sil, ril)
    tap_grad(1)
    taps_to_pair()
    point_over_z()
    taps_to_y()
    seg_wait(OM0, so.at[0], ro.at[0])
    seg_wait(OM1, so.at[1], ro.at[1])
    seg_wait(OL, sol, rol)
    taps_to_z()
    home(ro, rol, out_ref)
    taps_back_y()
    point_end()
    taps_back_pair()
    seg_wait(IM0, si.at[0], ri.at[0])
    seg_wait(IM1, si.at[1], ri.at[1])
    seg_wait(IL, sil, ril)
    home(ri, ril, gin_ref)
    taps_end()

    for j in range(2):
        seg_sent((XM0, XM1)[j], sx.at[j], rx.at[j])
        seg_sent((GM0, GM1)[j], sg.at[j], rg.at[j])
        seg_sent((OM0, OM1)[j], so.at[j], ro.at[j])
        seg_sent((IM0, IM1)[j], si.at[j], ri.at[j])
    seg_sent(XL, sxl, rxl)
    seg_sent(GL, sgl, rgl)
    seg_sent(OL, sol, rol)
    seg_sent(IL, sil, ril)
    for y in range(4):
        pair_copy(y).wait_send()
    tap_pair().wait_send()
    tap_back_pair(core).wait_send()
    for d in (1, 2, 3):
        y_copy(d).wait_send()
        z_copy(d).wait_send()
        tap_y(d).wait_send()
        tap_z(d, my_z).wait_send()
        tap_back_y(d, my_y).wait_send()


def body(feature_maps, path_lists, point_weight, depth_kernel, cotangent):
    x = feature_maps.transpose(1, 2, 0, 3).reshape(POS * 8, C)
    g = cotangent.transpose(1, 2, 0, 3).reshape(POS * 8, C)
    vmem = pl.BlockSpec(memory_space=pltpu.VMEM)
    main = pltpu.VMEM((2, SEG, MAIN, C), BF16)
    last = pltpu.VMEM((SEG, 16, LANES), BF16)
    wide = pltpu.VMEM((2, ROWS, C), F32)
    narrow = pltpu.VMEM((2, ROWS, C), BF16)
    out, gin, pgrad, dgrad = pl.pallas_call(
        kernel,
        out_shape=(
            jax.ShapeDtypeStruct((POS * 8, C), BF16),
            jax.ShapeDtypeStruct((POS * 8, C), BF16),
            jax.ShapeDtypeStruct((32, C), F32),
            jax.ShapeDtypeStruct((25, 1, C), F32),
        ),
        in_specs=[pl.BlockSpec(memory_space=pltpu.SMEM)] + [vmem] * 4,
        out_specs=[vmem] * 4,
        scratch_shapes=[
            *[main, main, last, last] * 4,
            wide, wide, wide, wide, narrow, narrow,
            pltpu.VMEM((2, ROWS, LANES), F32),
            pltpu.VMEM((25, 8, C), F32),
            pltpu.VMEM((128, LANES), F32),
            pltpu.VMEM((128, LANES), F32),
            pltpu.VMEM((4, 4, 2, 32, C), F32),
            pltpu.VMEM((4, 4, 32, C), F32),
            pltpu.VMEM((3, 4, 32, C), BF16),
            pltpu.VMEM((3, 4, 32, C), BF16),
            pltpu.VMEM((3, 32, C), BF16),
            pltpu.VMEM((3, 32, C), BF16),
            pltpu.VMEM((25, 8, C), F32),
            pltpu.VMEM((2, 4, 32, LANES), F32),
            pltpu.VMEM((4, 32, LANES), F32),
            pltpu.VMEM((3, 32, LANES), F32),
            pltpu.VMEM((4, 32, LANES), F32),
            pltpu.VMEM((2, 4, 32, LANES), F32),
            pltpu.SemaphoreType.DMA((12, SEG)),
            pltpu.SemaphoreType.DMA((12, SEG)),
            pltpu.SemaphoreType.DMA((12,)),
            pltpu.SemaphoreType.DMA((21,)),
            pltpu.SemaphoreType.DMA((21,)),
        ],
        compiler_params=pltpu.CompilerParams(
            collective_id=0, has_side_effects=True, vmem_limit_bytes=60 * 1024 * 1024
        ),
        name="supernet_window",
    )(path_lists[:, :, 0], x, g, point_weight[0, 0], depth_kernel[0].reshape(25, 1, C))
    final = out.reshape(SIDE, SIDE, 8, C).transpose(2, 0, 1, 3)
    grad = gin.reshape(SIDE, SIDE, 8, C).transpose(2, 0, 1, 3)
    return final, grad, pgrad[None, None], dgrad.reshape(1, 1, 25, C)


def solution(mesh):
    placed = (
        P(("segment", "rep"), None, None, None),
        P(None, ("segment", "rep"), None),
        P(None, "segment", None, None),
        P(None, "segment", None, None),
        P(("segment", "rep"), None, None, None),
    )
    return jax.shard_map(
        body,
        mesh=mesh,
        in_specs=placed,
        out_specs=(
            P(("segment", "rep"), None, None, None),
            P(("segment", "rep"), None, None, None),
            P(None, "segment", "rep", None),
            P(None, "segment", None, None),
        ),
        check_vma=False,
    )
```

```python
import functools

import jax
import jax.numpy as jnp
from jax import lax
from jax.experimental import pallas as pl
from jax.experimental.pallas import tpu as pltpu
from jax.sharding import PartitionSpec as P

MESH = pl.DeviceIdType.MESH
EPS = 1e-05
F32 = jnp.float32
BF16 = jnp.bfloat16

C = 1024
SIDE = 7
POS = SIDE * SIDE
MAIN = 48
ROWS = 400
LANES = 128
SEG = 8
PARTNERS = ((1, 0), (0, 1), (0, 3), (1, 1), (1, 3), (0, 2), (1, 2))

XM0, XM1, XL, GM0, GM1, GL, OM0, OM1, OL, IM0, IM1, IL = range(12)


def iota2(rows, cols):
    return (
        lax.broadcasted_iota(jnp.int32, (rows, cols), 0),
        lax.broadcasted_iota(jnp.int32, (rows, cols), 1),
    )


def onehot(cond):
    return jnp.where(cond, 1.0, 0.0)


def mm(a, b):
    return jnp.dot(a, b, preferred_element_type=F32)


def kernel(
    path_ref,
    x_in,
    g_in,
    w_in,
    k_in,
    out_hbm,
    gin_hbm,
    pgrad_ref,
    dgrad_ref,
    x_ref, g_ref, w_ref, k_ref, out_ref, gin_ref,
    sx, rx, sxl, rxl,
    sg, rg, sgl, rgl,
    so, ro, sol, rol,
    si, ri, sil, ril,
    x32, h32, gh32, g32, ab, gb, q128, kb,
    fold_o, fold_i,
    pg, prx, psb, prb, psc, prc,
    dka, tap_own, tap_pair_in, tap_y_in, tap_z_all, tap_all,
    send_sem, recv_sem, local_sem, rsend, rrecv, load_sem,
):
    me = lax.axis_index("segment")
    rep = lax.axis_index("rep")
    z_lo = me >> 2
    xx = me & 3
    my_y = rep >> 3
    my_z = (rep >> 1) & 3
    core = rep & 1

    def rep_at(dy, dz, dc):
        return (((my_y + dy) & 3) << 3) + (((my_z + dz) & 3) << 1) + ((core + dc) & 1)

    outside = rep_at(0, 2 * z_lo - 1, 0)

    def seg_at(dz, dx):
        return (((z_lo + dz) & 1) << 2) + ((xx + dx) & 3)

    def seg_device(dz, dx):
        return (seg_at(dz, dx), outside if dz and dx & 1 else rep)

    rep_partners = ((0, 0, 1), (1, 0, 0), (2, 0, 0), (3, 0, 0), (0, 1, 0), (0, 2, 0), (0, 3, 0))

    barrier = pltpu.get_barrier_semaphore()
    for dy, dz, dc in rep_partners:
        pl.semaphore_signal(
            barrier, inc=1, device_id=(me, rep_at(dy, dz, dc)), device_id_type=MESH
        )
    for dz, dx in PARTNERS:
        pl.semaphore_signal(barrier, inc=1, device_id=seg_device(dz, dx), device_id_type=MESH)

    loads = [
        pltpu.make_async_copy(far, near, load_sem.at[i])
        for i, (far, near) in enumerate(
            ((x_in, x_ref), (g_in, g_ref), (k_in, k_ref), (w_in, w_ref))
        )
    ]
    for load in loads:
        load.start()

    def seg_copy(kind, src, dst, dz, dx, received=False):
        there = seg_at(dz, dx)
        slot = there if received else me
        return pltpu.make_async_remote_copy(
            src_ref=src.at[there],
            dst_ref=dst.at[slot],
            send_sem=send_sem.at[kind, there],
            recv_sem=recv_sem.at[kind, slot],
            device_id=seg_device(dz, dx),
            device_id_type=MESH,
        )

    def seg_send(kind, src, dst):
        for dz, dx in PARTNERS:
            seg_copy(kind, src, dst, dz, dx).start()
        pltpu.make_async_copy(src.at[me], dst.at[me], local_sem.at[kind]).start()

    def seg_wait(kind, src, dst):
        pltpu.make_async_copy(src.at[me], dst.at[me], local_sem.at[kind]).wait()
        for dz, dx in PARTNERS:
            seg_copy(kind, src, dst, dz, dx, received=True).wait_recv()

    def seg_sent(kind, src, dst):
        for dz, dx in PARTNERS:
            seg_copy(kind, src, dst, dz, dx).wait_send()

    paths = [path_ref[0, i] for i in range(8)]
    slot_of = []
    for i in range(8):
        rank = jnp.int32(0)
        for earlier in range(i):
            rank = rank + jnp.where(paths[earlier] == paths[i], 1, 0)
        slot_of.append(2 * paths[i] + rank)

    def slots_like(sample):
        slots = jnp.full(sample.shape, -1, jnp.int32)
        for i in range(8):
            slots = jnp.where(sample == i, slot_of[i], slots)
        return slots

    m, n = iota2(256, 128)
    slots = slots_like(n & 7)
    wanted = 2 * ((m >> 4) & 7) + (m >> 7)
    route32 = onehot(((m & 15) == (n >> 3)) & (slots == wanted))
    route = route32.astype(BF16)
    route_back = route32.T.astype(BF16)
    m, n = iota2(128, 128)
    slots = slots_like(n & 7)
    route_last32 = onehot(((m & 7) == (n >> 3)) & (slots == (m >> 3)))
    route_last = route_last32.astype(BF16)
    route_last_back = route_last32.T.astype(BF16)
    to_rows = onehot(((m >> 3) == (n & 15)) & ((m & 7) == (n >> 4))).astype(BF16)
    from_rows = onehot(((m & 15) == (n >> 3)) & ((m >> 4) == (n & 7))).astype(BF16)
    unfold = onehot(
        ((m >> 4) == (n & 7)) & (((m >> 3) & 1) == ((n >> 3) & 1)) & ((m & 7) == (n >> 4))
    ).astype(BF16)
    refold = onehot(
        ((n >> 4) == (m & 7)) & (((n >> 3) & 1) == ((m >> 3) & 1)) & ((n & 7) == (m >> 4))
    ).astype(BF16)

    def dispatch(source, main, last):
        for q in range(3):
            for part in range(4):
                lanes = slice(part * 256, part * 256 + 256)
                moved = mm(route, source[q * 128 : q * 128 + 128, lanes]).astype(BF16)
                for j in range(2):
                    main[j, :, q * 16 : q * 16 + 16, lanes] = moved[
                        j * 128 : j * 128 + 128
                    ].reshape(8, 16, 256)
        tail = source[384:392, :].astype(F32)
        folded = jnp.concatenate(
            [tail[:, b * LANES : b * LANES + LANES] for b in range(8)]
            + [jnp.zeros((64, LANES), F32)],
            axis=0,
        ).astype(BF16)
        last[...] = mm(route_last, folded).astype(BF16).reshape(8, 16, LANES)

    loads[0].wait()
    dispatch(x_ref, sx, sxl)
    pl.semaphore_wait(barrier, 14)
    seg_send(XM0, sx.at[0], rx.at[0])
    seg_send(XL, sxl, rxl)
    loads[1].wait()
    dispatch(g_ref, sg, sgl)
    seg_send(GM0, sg.at[0], rg.at[0])
    seg_send(GL, sgl, rgl)
    seg_send(XM1, sx.at[1], rx.at[1])
    seg_send(GM1, sg.at[1], rg.at[1])

    loads[2].wait()
    kind = me % 3
    keep = []
    for t in range(25):
        row, col = t // 5 - 2, t % 5 - 2
        narrow = 1.0 if abs(row) <= 1 and abs(col) <= 1 else 0.0
        spaced = 1.0 if row % 2 == 0 and col % 2 == 0 else 0.0
        keep.append(jnp.where(kind == 0, narrow, jnp.where(kind == 1, 1.0, spaced)))
        kb[t] = jnp.broadcast_to(k_ref[t], (8, C)) * keep[t]
    dka[...] = jnp.zeros((25, 8, C), F32)
    for j in range(2):
        x32[j, 392:400, :] = jnp.zeros((8, C), F32)
        h32[j, 392:400, :] = jnp.zeros((8, C), F32)

    def receive_main(j, got, wide, narrow):
        for q in range(3):
            for part in range(4):
                lanes = slice(part * 256, part * 256 + 256)
                rows = mm(to_rows, got[j, :, q * 16 : q * 16 + 16, lanes].reshape(128, 256))
                wide[j, q * 128 : q * 128 + 128, lanes] = rows
                if narrow is not None:
                    narrow[j, q * 128 : q * 128 + 128, lanes] = rows.astype(BF16)

    def receive_last(got, wide, narrow):
        rows = mm(unfold, got[...].reshape(128, LANES))
        for j in range(2):
            row = jnp.concatenate(
                [rows[b * 16 + j * 8 : b * 16 + j * 8 + 8] for b in range(8)], axis=1
            )
            wide[j, 384:392, :] = row
            if narrow is not None:
                narrow[j, 384:400, :] = jnp.concatenate([row, jnp.zeros((8, C), F32)], 0).astype(BF16)

    def rows_at(ref, j, r, lanes):
        return [ref[j, (r * 7 + c) * 8 : (r * 7 + c) * 8 + 8, lanes] for c in range(7)]

    def convolve(j, source, sign, emit):
        def body(block, carry):
            lanes = pl.ds(pl.multiple_of(block * LANES, LANES), LANES)
            for r in range(7):
                acc = [None] * 7
                for dr in range(-2, 3):
                    at = r + sign * dr
                    if at < 0 or at > 6:
                        continue
                    row = rows_at(source, j, at, lanes)
                    for dc in range(-2, 3):
                        tap = kb[(dr + 2) * 5 + dc + 2, :, lanes]
                        for c in range(7):
                            ac = c + sign * dc
                            if ac < 0 or ac > 6:
                                continue
                            term = tap * row[ac]
                            acc[c] = term if acc[c] is None else acc[c] + term
                for c in range(7):
                    emit(j, (r * 7 + c) * 8, lanes, acc[c])
            return carry

        lax.fori_loop(0, 8, body, 0)

    def emit_h(j, row, lanes, value):
        h32[j, row : row + 8, lanes] = value

    def emit_gin(j, row, lanes, value):
        g32[j, row : row + 8, lanes] = g32[j, row : row + 8, lanes] + value

    def tap_grad(j):
        def body(block, carry):
            lanes = pl.ds(pl.multiple_of(block * LANES, LANES), LANES)
            for dr in range(-2, 3):
                acc = [None] * 5
                for r in range(7):
                    at = r + dr
                    if at < 0 or at > 6:
                        continue
                    grad = rows_at(gh32, j, r, lanes)
                    row = rows_at(x32, j, at, lanes)
                    for dc in range(-2, 3):
                        for c in range(7):
                            ac = c + dc
                            if ac < 0 or ac > 6:
                                continue
                            term = grad[c] * row[ac]
                            acc[dc + 2] = term if acc[dc + 2] is None else acc[dc + 2] + term
                for t in range(5):
                    at = (dr + 2) * 5 + t
                    dka[at, :, lanes] = dka[at, :, lanes] + acc[t]
            return carry

        lax.fori_loop(0, 8, body, 0)

    def activate(j):
        def body(step, carry):
            rows = pl.ds(pl.multiple_of(step * 80, 80), 80)
            h = h32[j, rows, :]
            q = lax.rsqrt(jnp.sum(h * h, axis=1, keepdims=True) * (1.0 / C) + EPS)
            z = h * q
            h32[j, rows, :] = z
            q128[j, rows, :] = jnp.broadcast_to(q, (80, LANES))
            ab[j, rows, :] = (z * jax.nn.sigmoid(z)).astype(BF16)
            return carry

        lax.fori_loop(0, 5, body, 0)

    def send_rows(j, value, n, main, fold):
        lanes = pl.ds(pl.multiple_of(n * 256, 256), 256)
        for q in range(3):
            moved = mm(from_rows, value[q * 128 : q * 128 + 128]).astype(BF16)
            main[j, :, q * 16 : q * 16 + 16, lanes] = moved.reshape(8, 16, 256)
        tail = value[384:400].astype(F32)
        for b in range(2):
            fold[pl.ds(pl.multiple_of((2 * n + b) * 16 + j * 8, 8), 8), :] = tail[
                :8, b * LANES : b * LANES + LANES
            ]

    def send_last(fold, last):
        last[...] = mm(refold, fold[...].astype(BF16)).astype(BF16).reshape(8, 16, LANES)

    def project(j):
        def body(n, carry):
            lanes = pl.ds(pl.multiple_of(n * 256, 256), 256)
            value = (x32[j, :, lanes] + mm(ab[j], w_ref[:, lanes])).astype(BF16)
            send_rows(j, value, n, so, fold_o)
            return carry

        lax.fori_loop(0, 4, body, 0)

    def back_project(j):
        def body(n, carry):
            lanes = pl.ds(pl.multiple_of(n * 256, 256), 256)
            gh32[j, :, lanes] = lax.dot_general(
                gb[j], w_ref[lanes, :], (((1,), (1,)), ((), ())), preferred_element_type=F32
            )
            return carry

        lax.fori_loop(0, 4, body, 0)

    def back_activate(j):
        def body(step, carry):
            rows = pl.ds(pl.multiple_of(step * 80, 80), 80)
            z = h32[j, rows, :]
            s = jax.nn.sigmoid(z)
            gz = gh32[j, rows, :] * s * (1.0 + z * (1.0 - s))
            mean = jnp.sum(gz * z, axis=1, keepdims=True) * (1.0 / C)
            q = jnp.concatenate([q128[j, rows, :]] * 8, axis=1)
            gh32[j, rows, :] = q * (gz - z * mean)
            return carry

        lax.fori_loop(0, 5, body, 0)

    def send_gin(j):
        def body(n, carry):
            lanes = pl.ds(pl.multiple_of(n * 256, 256), 256)
            send_rows(j, g32[j, :, lanes].astype(BF16), n, si, fold_i)
            return carry

        lax.fori_loop(0, 4, body, 0)

    def forward(j):
        seg_wait((XM0, XM1)[j], sx.at[j], rx.at[j])
        receive_main(j, rx, x32, None)
        if j == 0:
            seg_wait(XL, sxl, rxl)
            receive_last(rxl, x32, None)
        convolve(j, x32, 1, emit_h)
        activate(j)
        project(j)
        seg_send((OM0, OM1)[j], so.at[j], ro.at[j])
        if j == 1:
            send_last(fold_o, sol)
            seg_send(OL, sol, rol)

    def receive_g(j):
        seg_wait((GM0, GM1)[j], sg.at[j], rg.at[j])
        receive_main(j, rg, g32, gb)
        if j == 0:
            seg_wait(GL, sgl, rgl)
            receive_last(rgl, g32, gb)
            for i in range(2):
                g32[i, 392:400, :] = jnp.zeros((8, C), F32)

    def backward(j):
        back_project(j)
        back_activate(j)
        convolve(j, gh32, -1, emit_gin)
        send_gin(j)
        seg_send((IM0, IM1)[j], si.at[j], ri.at[j])

    def home(main, last, target):
        for q in range(3):
            for part in range(4):
                lanes = slice(part * 256, part * 256 + 256)
                got = jnp.concatenate(
                    [main[j, :, q * 16 : q * 16 + 16, lanes].reshape(128, 256) for j in range(2)],
                    axis=0,
                )
                target[q * 128 : q * 128 + 128, lanes] = mm(route_back, got).astype(BF16)
        rows = mm(route_last_back, last[...].reshape(128, LANES))
        target[384:392, :] = jnp.concatenate(
            [rows[b * 8 : b * 8 + 8] for b in range(8)], axis=1
        ).astype(BF16)

    def rep_copy(kind, src, dst, dy, dz, dc):
        return pltpu.make_async_remote_copy(
            src_ref=src,
            dst_ref=dst,
            send_sem=rsend.at[kind],
            recv_sem=rrecv.at[kind],
            device_id=(me, rep_at(dy, dz, dc)),
            device_id_type=MESH,
        )

    sibling = 1 - core

    def pair_copy(y):
        return rep_copy(y, pg.at[y, :, sibling], prx.at[y], 0, 0, 1)

    def point_terms(j):
        for dy in (1, 2, 3, 0):
            y = (my_y + dy) & 3
            cols = pl.ds(pl.multiple_of(y * 256, 256), 256)
            for part in range(4):
                lanes = slice(part * 256, part * 256 + 256)
                term = lax.dot_general(
                    ab[j, :, cols],
                    gb[j, :, lanes],
                    (((0,), (0,)), ((), ())),
                    preferred_element_type=F32,
                ).reshape(4, 2, 32, 256)
                if j == 0:
                    pg[y, :, :, :, lanes] = term
                else:
                    pg[y, :, :, :, lanes] = pg[y, :, :, :, lanes] + term
            if j == 1:
                pair_copy(y).start()

    def y_copy(dy):
        return rep_copy(3 + dy, psb.at[dy - 1], prb.at[dy - 1], dy, 0, 0)

    def z_copy(dz):
        return rep_copy(6 + dz, psc.at[dz - 1], prc.at[dz - 1], 0, dz, 0)

    def point_over_y():
        for dy in (1, 2, 3, 0):
            y = (my_y + dy) & 3
            pair_copy(y).wait_recv()
            total = pg[y, :, core] + prx[y]
            if dy:
                psb[dy - 1] = total.astype(BF16)
                y_copy(dy).start()
            else:
                prx[y] = total

    def point_over_z():
        total = prx[my_y]
        for dy in (1, 2, 3):
            y_copy(dy).wait_recv()
        for slot in range(3):
            total = total + prb[slot].astype(F32)
        prx[my_y] = total
        for dz in (1, 2, 3):
            psc[dz - 1] = prx[my_y, (my_z + dz) & 3].astype(BF16)
            z_copy(dz).start()

    def point_end():
        for dz in (1, 2, 3):
            z_copy(dz).wait_recv()
        total = prx[my_y, my_z]
        for slot in range(3):
            total = total + prc[slot].astype(F32)
        pgrad_ref[...] = total

    def tap_pair():
        return rep_copy(10, tap_own.at[sibling], tap_pair_in, 0, 0, 1)

    def tap_y(dy):
        return rep_copy(10 + dy, tap_own.at[core, (my_y + dy) & 3], tap_y_in.at[dy - 1], dy, 0, 0)

    def tap_z(dz, slot):
        return rep_copy(13 + dz, tap_z_all.at[my_z], tap_z_all.at[slot], 0, dz, 0)

    def tap_back_y(dy, slot):
        return rep_copy(16 + dy, tap_all.at[core, my_y], tap_all.at[core, slot], dy, 0, 0)

    def tap_back_pair(slot):
        return rep_copy(20, tap_all.at[core], tap_all.at[slot], 0, 0, 1)

    def taps_to_pair():
        sums = jnp.concatenate([jnp.sum(dka[...], axis=1), jnp.zeros((7, C), F32)], axis=0)
        for block in range(8):
            tap_own[block // 4, block & 3] = sums[:, block * LANES : block * LANES + LANES]
        tap_pair().start()

    def taps_to_y():
        tap_pair().wait_recv()
        tap_own[core] = tap_own[core] + tap_pair_in[...]
        for dy in (1, 2, 3):
            tap_y(dy).start()

    def taps_to_z():
        total = tap_own[core, my_y]
        for dy in (1, 2, 3):
            tap_y(dy).wait_recv()
            total = total + tap_y_in[dy - 1]
        tap_z_all[my_z] = total
        for dz in (1, 2, 3):
            tap_z(dz, my_z).start()

    def taps_back_y():
        for dz in (1, 2, 3):
            tap_z(dz, (my_z + 4 - dz) & 3).wait_recv()
        tap_all[core, my_y] = (tap_z_all[0] + tap_z_all[1]) + (tap_z_all[2] + tap_z_all[3])
        for dy in (1, 2, 3):
            tap_back_y(dy, my_y).start()

    def taps_back_pair():
        for dy in (1, 2, 3):
            tap_back_y(dy, (my_y + 4 - dy) & 3).wait_recv()
        tap_back_pair(core).start()

    def taps_end():
        tap_back_pair(sibling).wait_recv()
        sums = jnp.concatenate([tap_all[b // 4, b & 3] for b in range(8)], axis=1)
        for t in range(25):
            dgrad_ref[t] = sums[t : t + 1] * keep[t]

    loads[3].wait()
    forward(0)
    receive_g(0)
    backward(0)
    tap_grad(0)
    point_terms(0)
    forward(1)
    receive_g(1)
    point_terms(1)
    back_project(1)
    back_activate(1)
    point_over_y()
    convolve(1, gh32, -1, emit_gin)
    send_gin(1)
    seg_send(IM1, si.at[1], ri.at[1])
    send_last(fold_i, sil)
    seg_send(IL, sil, ril)
    tap_grad(1)
    taps_to_pair()
    point_over_z()
    taps_to_y()
    seg_wait(OM0, so.at[0], ro.at[0])
    seg_wait(OM1, so.at[1], ro.at[1])
    seg_wait(OL, sol, rol)
    taps_to_z()
    home(ro, rol, out_ref)
    store_out = pltpu.make_async_copy(out_ref, out_hbm, load_sem.at[4])
    store_out.start()
    taps_back_y()
    point_end()
    taps_back_pair()
    seg_wait(IM0, si.at[0], ri.at[0])
    seg_wait(IM1, si.at[1], ri.at[1])
    seg_wait(IL, sil, ril)
    home(ri, ril, gin_ref)
    store_gin = pltpu.make_async_copy(gin_ref, gin_hbm, load_sem.at[5])
    store_gin.start()
    taps_end()

    for j in range(2):
        seg_sent((XM0, XM1)[j], sx.at[j], rx.at[j])
        seg_sent((GM0, GM1)[j], sg.at[j], rg.at[j])
        seg_sent((OM0, OM1)[j], so.at[j], ro.at[j])
        seg_sent((IM0, IM1)[j], si.at[j], ri.at[j])
    seg_sent(XL, sxl, rxl)
    seg_sent(GL, sgl, rgl)
    seg_sent(OL, sol, rol)
    seg_sent(IL, sil, ril)
    for y in range(4):
        pair_copy(y).wait_send()
    tap_pair().wait_send()
    tap_back_pair(core).wait_send()
    for d in (1, 2, 3):
        y_copy(d).wait_send()
        z_copy(d).wait_send()
        tap_y(d).wait_send()
        tap_z(d, my_z).wait_send()
        tap_back_y(d, my_y).wait_send()
    store_out.wait()
    store_gin.wait()


def body(feature_maps, path_lists, point_weight, depth_kernel, cotangent):
    x = feature_maps.transpose(1, 2, 0, 3).reshape(POS * 8, C)
    g = cotangent.transpose(1, 2, 0, 3).reshape(POS * 8, C)
    vmem = pl.BlockSpec(memory_space=pltpu.VMEM)
    anywhere = pl.BlockSpec(memory_space=pl.ANY)
    maps = pltpu.VMEM((POS * 8, C), BF16)
    main = pltpu.VMEM((2, SEG, MAIN, C), BF16)
    last = pltpu.VMEM((SEG, 16, LANES), BF16)
    wide = pltpu.VMEM((2, ROWS, C), F32)
    narrow = pltpu.VMEM((2, ROWS, C), BF16)
    out, gin, pgrad, dgrad = pl.pallas_call(
        kernel,
        out_shape=(
            jax.ShapeDtypeStruct((POS * 8, C), BF16),
            jax.ShapeDtypeStruct((POS * 8, C), BF16),
            jax.ShapeDtypeStruct((32, C), F32),
            jax.ShapeDtypeStruct((25, 1, C), F32),
        ),
        in_specs=[pl.BlockSpec(memory_space=pltpu.SMEM)] + [anywhere] * 4,
        out_specs=[anywhere] * 2 + [vmem] * 2,
        scratch_shapes=[
            maps, maps, pltpu.VMEM((C, C), BF16), pltpu.VMEM((25, 1, C), F32), maps, maps,
            *[main, main, last, last] * 4,
            wide, wide, wide, wide, narrow, narrow,
            pltpu.VMEM((2, ROWS, LANES), F32),
            pltpu.VMEM((25, 8, C), F32),
            pltpu.VMEM((128, LANES), F32),
            pltpu.VMEM((128, LANES), F32),
            pltpu.VMEM((4, 4, 2, 32, C), F32),
            pltpu.VMEM((4, 4, 32, C), F32),
            pltpu.VMEM((3, 4, 32, C), BF16),
            pltpu.VMEM((3, 4, 32, C), BF16),
            pltpu.VMEM((3, 32, C), BF16),
            pltpu.VMEM((3, 32, C), BF16),
            pltpu.VMEM((25, 8, C), F32),
            pltpu.VMEM((2, 4, 32, LANES), F32),
            pltpu.VMEM((4, 32, LANES), F32),
            pltpu.VMEM((3, 32, LANES), F32),
            pltpu.VMEM((4, 32, LANES), F32),
            pltpu.VMEM((2, 4, 32, LANES), F32),
            pltpu.SemaphoreType.DMA((12, SEG)),
            pltpu.SemaphoreType.DMA((12, SEG)),
            pltpu.SemaphoreType.DMA((12,)),
            pltpu.SemaphoreType.DMA((21,)),
            pltpu.SemaphoreType.DMA((21,)),
            pltpu.SemaphoreType.DMA((6,)),
        ],
        compiler_params=pltpu.CompilerParams(
            collective_id=0, has_side_effects=True, vmem_limit_bytes=60 * 1024 * 1024
        ),
        name="supernet_window",
    )(path_lists[:, :, 0], x, g, point_weight[0, 0], depth_kernel[0].reshape(25, 1, C))
    final = out.reshape(SIDE, SIDE, 8, C).transpose(2, 0, 1, 3)
    grad = gin.reshape(SIDE, SIDE, 8, C).transpose(2, 0, 1, 3)
    return final, grad, pgrad[None, None], dgrad.reshape(1, 1, 25, C)


def solution(mesh):
    placed = (
        P(("segment", "rep"), None, None, None),
        P(None, ("segment", "rep"), None),
        P(None, "segment", None, None),
        P(None, "segment", None, None),
        P(("segment", "rep"), None, None, None),
    )
    return jax.shard_map(
        body,
        mesh=mesh,
        in_specs=placed,
        out_specs=(
            P(("segment", "rep"), None, None, None),
            P(("segment", "rep"), None, None, None),
            P(None, "segment", "rep", None),
            P(None, "segment", None, None),
        ),
        check_vma=False,
    )
```

```python
import functools

import jax
import jax.numpy as jnp
from jax import lax
from jax.experimental import pallas as pl
from jax.experimental.pallas import tpu as pltpu
from jax.sharding import PartitionSpec as P

MESH = pl.DeviceIdType.MESH
EPS = 1e-05
F32 = jnp.float32
BF16 = jnp.bfloat16

C = 1024
SIDE = 7
POS = SIDE * SIDE
MAIN = 48
ROWS = 400
LANES = 128
SEG = 8
PARTNERS = ((0, 2), (1, 2), (0, 1), (0, 3), (1, 1), (1, 3), (1, 0))

XM0, XM1, XL, GM0, GM1, GL, OM0, OM1, OL, IM0, IM1, IL = range(12)


def iota2(rows, cols):
    return (
        lax.broadcasted_iota(jnp.int32, (rows, cols), 0),
        lax.broadcasted_iota(jnp.int32, (rows, cols), 1),
    )


def onehot(cond):
    return jnp.where(cond, 1.0, 0.0)


def mm(a, b):
    return jnp.dot(a, b, preferred_element_type=F32)


def kernel(
    path_ref,
    x_in,
    g_in,
    w_in,
    k_in,
    out_hbm,
    gin_hbm,
    pgrad_ref,
    dgrad_ref,
    x_ref, g_ref, w_ref, k_ref, out_ref, gin_ref,
    sx, rx, sxl, rxl,
    sg, rg, sgl, rgl,
    so, ro, sol, rol,
    si, ri, sil, ril,
    x32, h32, gh32, g32, ab, gb, q128, kb,
    fold_o, fold_i,
    pg, prx, psb, prb, psc, prc,
    dka, tap_own, tap_pair_in, tap_y_in, tap_z_all, tap_all,
    send_sem, recv_sem, local_sem, rsend, rrecv, load_sem,
):
    me = lax.axis_index("segment")
    rep = lax.axis_index("rep")
    z_lo = me >> 2
    xx = me & 3
    my_y = rep >> 3
    my_z = (rep >> 1) & 3
    core = rep & 1

    def rep_at(dy, dz, dc):
        return (((my_y + dy) & 3) << 3) + (((my_z + dz) & 3) << 1) + ((core + dc) & 1)

    outside = rep_at(0, 2 * z_lo - 1, 0)

    def seg_at(dz, dx):
        return (((z_lo + dz) & 1) << 2) + ((xx + dx) & 3)

    def seg_device(dz, dx):
        return (seg_at(dz, dx), outside if dz and dx & 1 else rep)

    rep_partners = ((0, 0, 1), (1, 0, 0), (2, 0, 0), (3, 0, 0), (0, 1, 0), (0, 2, 0), (0, 3, 0))

    barrier = pltpu.get_barrier_semaphore()
    for dy, dz, dc in rep_partners:
        pl.semaphore_signal(
            barrier, inc=1, device_id=(me, rep_at(dy, dz, dc)), device_id_type=MESH
        )
    for dz, dx in PARTNERS:
        pl.semaphore_signal(barrier, inc=1, device_id=seg_device(dz, dx), device_id_type=MESH)

    loads = [
        pltpu.make_async_copy(far, near, load_sem.at[i])
        for i, (far, near) in enumerate(
            ((x_in, x_ref), (g_in, g_ref), (k_in, k_ref), (w_in, w_ref))
        )
    ]
    for load in loads:
        load.start()

    def seg_copy(kind, src, dst, dz, dx, received=False):
        there = seg_at(dz, dx)
        slot = there if received else me
        return pltpu.make_async_remote_copy(
            src_ref=src.at[there],
            dst_ref=dst.at[slot],
            send_sem=send_sem.at[kind, there],
            recv_sem=recv_sem.at[kind, slot],
            device_id=seg_device(dz, dx),
            device_id_type=MESH,
        )

    def seg_send(kind, src, dst):
        for dz, dx in PARTNERS:
            seg_copy(kind, src, dst, dz, dx).start()
        pltpu.make_async_copy(src.at[me], dst.at[me], local_sem.at[kind]).start()

    def seg_wait(kind, src, dst):
        pltpu.make_async_copy(src.at[me], dst.at[me], local_sem.at[kind]).wait()
        for dz, dx in PARTNERS:
            seg_copy(kind, src, dst, dz, dx, received=True).wait_recv()

    def seg_sent(kind, src, dst):
        for dz, dx in PARTNERS:
            seg_copy(kind, src, dst, dz, dx).wait_send()

    paths = [path_ref[0, i] for i in range(8)]
    slot_of = []
    for i in range(8):
        rank = jnp.int32(0)
        for earlier in range(i):
            rank = rank + jnp.where(paths[earlier] == paths[i], 1, 0)
        slot_of.append(2 * paths[i] + rank)

    def slots_like(sample):
        slots = jnp.full(sample.shape, -1, jnp.int32)
        for i in range(8):
            slots = jnp.where(sample == i, slot_of[i], slots)
        return slots

    m, n = iota2(256, 128)
    slots = slots_like(n & 7)
    wanted = 2 * ((m >> 4) & 7) + (m >> 7)
    route32 = onehot(((m & 15) == (n >> 3)) & (slots == wanted))
    route = route32.astype(BF16)
    route_back = route32.T.astype(BF16)
    m, n = iota2(128, 128)
    slots = slots_like(n & 7)
    route_last32 = onehot(((m & 7) == (n >> 3)) & (slots == (m >> 3)))
    route_last = route_last32.astype(BF16)
    route_last_back = route_last32.T.astype(BF16)
    to_rows = onehot(((m >> 3) == (n & 15)) & ((m & 7) == (n >> 4))).astype(BF16)
    from_rows = onehot(((m & 15) == (n >> 3)) & ((m >> 4) == (n & 7))).astype(BF16)
    unfold = onehot(
        ((m >> 4) == (n & 7)) & (((m >> 3) & 1) == ((n >> 3) & 1)) & ((m & 7) == (n >> 4))
    ).astype(BF16)
    refold = onehot(
        ((n >> 4) == (m & 7)) & (((n >> 3) & 1) == ((m >> 3) & 1)) & ((n & 7) == (m >> 4))
    ).astype(BF16)

    def dispatch(source, main, last):
        for q in range(3):
            for part in range(4):
                lanes = slice(part * 256, part * 256 + 256)
                moved = mm(route, source[q * 128 : q * 128 + 128, lanes]).astype(BF16)
                for j in range(2):
                    main[j, :, q * 16 : q * 16 + 16, lanes] = moved[
                        j * 128 : j * 128 + 128
                    ].reshape(8, 16, 256)
        tail = source[384:392, :].astype(F32)
        folded = jnp.concatenate(
            [tail[:, b * LANES : b * LANES + LANES] for b in range(8)]
            + [jnp.zeros((64, LANES), F32)],
            axis=0,
        ).astype(BF16)
        last[...] = mm(route_last, folded).astype(BF16).reshape(8, 16, LANES)

    loads[0].wait()
    dispatch(x_ref, sx, sxl)
    pl.semaphore_wait(barrier, 14)
    seg_send(XM0, sx.at[0], rx.at[0])
    seg_send(XL, sxl, rxl)
    loads[1].wait()
    dispatch(g_ref, sg, sgl)
    seg_send(GM0, sg.at[0], rg.at[0])
    seg_send(GL, sgl, rgl)
    seg_send(XM1, sx.at[1], rx.at[1])
    seg_send(GM1, sg.at[1], rg.at[1])

    loads[2].wait()
    kind = me % 3
    keep = []
    for t in range(25):
        row, col = t // 5 - 2, t % 5 - 2
        narrow = 1.0 if abs(row) <= 1 and abs(col) <= 1 else 0.0
        spaced = 1.0 if row % 2 == 0 and col % 2 == 0 else 0.0
        keep.append(jnp.where(kind == 0, narrow, jnp.where(kind == 1, 1.0, spaced)))
        kb[t] = jnp.broadcast_to(k_ref[t], (8, C)) * keep[t]
    dka[...] = jnp.zeros((25, 8, C), F32)
    for j in range(2):
        x32[j, 392:400, :] = jnp.zeros((8, C), F32)
        h32[j, 392:400, :] = jnp.zeros((8, C), F32)

    def receive_main(j, got, wide, narrow):
        for q in range(3):
            for part in range(4):
                lanes = slice(part * 256, part * 256 + 256)
                rows = mm(to_rows, got[j, :, q * 16 : q * 16 + 16, lanes].reshape(128, 256))
                wide[j, q * 128 : q * 128 + 128, lanes] = rows
                if narrow is not None:
                    narrow[j, q * 128 : q * 128 + 128, lanes] = rows.astype(BF16)

    def receive_last(got, wide, narrow):
        rows = mm(unfold, got[...].reshape(128, LANES))
        for j in range(2):
            row = jnp.concatenate(
                [rows[b * 16 + j * 8 : b * 16 + j * 8 + 8] for b in range(8)], axis=1
            )
            wide[j, 384:392, :] = row
            if narrow is not None:
                narrow[j, 384:400, :] = jnp.concatenate([row, jnp.zeros((8, C), F32)], 0).astype(BF16)

    def rows_at(ref, j, r, lanes):
        return [ref[j, (r * 7 + c) * 8 : (r * 7 + c) * 8 + 8, lanes] for c in range(7)]

    def convolve(j, source, sign, emit):
        def body(block, carry):
            lanes = pl.ds(pl.multiple_of(block * LANES, LANES), LANES)
            for r in range(7):
                acc = [None] * 7
                for dr in range(-2, 3):
                    at = r + sign * dr
                    if at < 0 or at > 6:
                        continue
                    row = rows_at(source, j, at, lanes)
                    for dc in range(-2, 3):
                        tap = kb[(dr + 2) * 5 + dc + 2, :, lanes]
                        for c in range(7):
                            ac = c + sign * dc
                            if ac < 0 or ac > 6:
                                continue
                            term = tap * row[ac]
                            acc[c] = term if acc[c] is None else acc[c] + term
                for c in range(7):
                    emit(j, (r * 7 + c) * 8, lanes, acc[c])
            return carry

        lax.fori_loop(0, 8, body, 0)

    def emit_h(j, row, lanes, value):
        h32[j, row : row + 8, lanes] = value

    def emit_gin(j, row, lanes, value):
        g32[j, row : row + 8, lanes] = g32[j, row : row + 8, lanes] + value

    def tap_grad(j):
        def body(block, carry):
            lanes = pl.ds(pl.multiple_of(block * LANES, LANES), LANES)
            for dr in range(-2, 3):
                acc = [None] * 5
                for r in range(7):
                    at = r + dr
                    if at < 0 or at > 6:
                        continue
                    grad = rows_at(gh32, j, r, lanes)
                    row = rows_at(x32, j, at, lanes)
                    for dc in range(-2, 3):
                        for c in range(7):
                            ac = c + dc
                            if ac < 0 or ac > 6:
                                continue
                            term = grad[c] * row[ac]
                            acc[dc + 2] = term if acc[dc + 2] is None else acc[dc + 2] + term
                for t in range(5):
                    at = (dr + 2) * 5 + t
                    dka[at, :, lanes] = dka[at, :, lanes] + acc[t]
            return carry

        lax.fori_loop(0, 8, body, 0)

    def activate(j):
        def body(step, carry):
            rows = pl.ds(pl.multiple_of(step * 80, 80), 80)
            h = h32[j, rows, :]
            q = lax.rsqrt(jnp.sum(h * h, axis=1, keepdims=True) * (1.0 / C) + EPS)
            z = h * q
            h32[j, rows, :] = z
            q128[j, rows, :] = jnp.broadcast_to(q, (80, LANES))
            ab[j, rows, :] = (z * jax.nn.sigmoid(z)).astype(BF16)
            return carry

        lax.fori_loop(0, 5, body, 0)

    def send_rows(j, value, n, main, fold):
        lanes = pl.ds(pl.multiple_of(n * 256, 256), 256)
        for q in range(3):
            moved = mm(from_rows, value[q * 128 : q * 128 + 128]).astype(BF16)
            main[j, :, q * 16 : q * 16 + 16, lanes] = moved.reshape(8, 16, 256)
        tail = value[384:400].astype(F32)
        for b in range(2):
            fold[pl.ds(pl.multiple_of((2 * n + b) * 16 + j * 8, 8), 8), :] = tail[
                :8, b * LANES : b * LANES + LANES
            ]

    def send_last(fold, last):
        last[...] = mm(refold, fold[...].astype(BF16)).astype(BF16).reshape(8, 16, LANES)

    def project(j):
        def body(n, carry):
            lanes = pl.ds(pl.multiple_of(n * 256, 256), 256)
            value = (x32[j, :, lanes] + mm(ab[j], w_ref[:, lanes])).astype(BF16)
            send_rows(j, value, n, so, fold_o)
            return carry

        lax.fori_loop(0, 4, body, 0)

    def back_project(j):
        def body(n, carry):
            lanes = pl.ds(pl.multiple_of(n * 256, 256), 256)
            gh32[j, :, lanes] = lax.dot_general(
                gb[j], w_ref[lanes, :], (((1,), (1,)), ((), ())), preferred_element_type=F32
            )
            return carry

        lax.fori_loop(0, 4, body, 0)

    def back_activate(j):
        def body(step, carry):
            rows = pl.ds(pl.multiple_of(step * 80, 80), 80)
            z = h32[j, rows, :]
            s = jax.nn.sigmoid(z)
            gz = gh32[j, rows, :] * s * (1.0 + z * (1.0 - s))
            mean = jnp.sum(gz * z, axis=1, keepdims=True) * (1.0 / C)
            q = jnp.concatenate([q128[j, rows, :]] * 8, axis=1)
            gh32[j, rows, :] = q * (gz - z * mean)
            return carry

        lax.fori_loop(0, 5, body, 0)

    def send_gin(j):
        def body(n, carry):
            lanes = pl.ds(pl.multiple_of(n * 256, 256), 256)
            send_rows(j, g32[j, :, lanes].astype(BF16), n, si, fold_i)
            return carry

        lax.fori_loop(0, 4, body, 0)

    def forward(j):
        seg_wait((XM0, XM1)[j], sx.at[j], rx.at[j])
        receive_main(j, rx, x32, None)
        if j == 0:
            seg_wait(XL, sxl, rxl)
            receive_last(rxl, x32, None)
        convolve(j, x32, 1, emit_h)
        activate(j)
        project(j)
        seg_send((OM0, OM1)[j], so.at[j], ro.at[j])
        if j == 1:
            send_last(fold_o, sol)
            seg_send(OL, sol, rol)

    def receive_g(j):
        seg_wait((GM0, GM1)[j], sg.at[j], rg.at[j])
        receive_main(j, rg, g32, gb)
        if j == 0:
            seg_wait(GL, sgl, rgl)
            receive_last(rgl, g32, gb)
            for i in range(2):
                g32[i, 392:400, :] = jnp.zeros((8, C), F32)

    def backward(j):
        back_project(j)
        back_activate(j)
        convolve(j, gh32, -1, emit_gin)
        send_gin(j)
        seg_send((IM0, IM1)[j], si.at[j], ri.at[j])

    def home(main, last, target):
        for q in range(3):
            for part in range(4):
                lanes = slice(part * 256, part * 256 + 256)
                got = jnp.concatenate(
                    [main[j, :, q * 16 : q * 16 + 16, lanes].reshape(128, 256) for j in range(2)],
                    axis=0,
                )
                target[q * 128 : q * 128 + 128, lanes] = mm(route_back, got).astype(BF16)
        rows = mm(route_last_back, last[...].reshape(128, LANES))
        target[384:392, :] = jnp.concatenate(
            [rows[b * 8 : b * 8 + 8] for b in range(8)], axis=1
        ).astype(BF16)

    def rep_copy(kind, src, dst, dy, dz, dc):
        return pltpu.make_async_remote_copy(
            src_ref=src,
            dst_ref=dst,
            send_sem=rsend.at[kind],
            recv_sem=rrecv.at[kind],
            device_id=(me, rep_at(dy, dz, dc)),
            device_id_type=MESH,
        )

    sibling = 1 - core

    def pair_copy(y):
        return rep_copy(y, pg.at[y, :, sibling], prx.at[y], 0, 0, 1)

    def point_terms(j):
        for dy in (1, 2, 3, 0):
            y = (my_y + dy) & 3
            cols = pl.ds(pl.multiple_of(y * 256, 256), 256)
            for part in range(4):
                lanes = slice(part * 256, part * 256 + 256)
                term = lax.dot_general(
                    ab[j, :, cols],
                    gb[j, :, lanes],
                    (((0,), (0,)), ((), ())),
                    preferred_element_type=F32,
                ).reshape(4, 2, 32, 256)
                if j == 0:
                    pg[y, :, :, :, lanes] = term
                else:
                    pg[y, :, :, :, lanes] = pg[y, :, :, :, lanes] + term
            if j == 1:
                pair_copy(y).start()

    def y_copy(dy):
        return rep_copy(3 + dy, psb.at[dy - 1], prb.at[dy - 1], dy, 0, 0)

    def z_copy(dz):
        return rep_copy(6 + dz, psc.at[dz - 1], prc.at[dz - 1], 0, dz, 0)

    def point_over_y():
        for dy in (1, 2, 3, 0):
            y = (my_y + dy) & 3
            pair_copy(y).wait_recv()
            total = pg[y, :, core] + prx[y]
            if dy:
                psb[dy - 1] = total.astype(BF16)
                y_copy(dy).start()
            else:
                prx[y] = total

    def point_over_z():
        total = prx[my_y]
        for dy in (1, 2, 3):
            y_copy(dy).wait_recv()
        for slot in range(3):
            total = total + prb[slot].astype(F32)
        prx[my_y] = total
        for dz in (1, 2, 3):
            psc[dz - 1] = prx[my_y, (my_z + dz) & 3].astype(BF16)
            z_copy(dz).start()

    def point_end():
        for dz in (1, 2, 3):
            z_copy(dz).wait_recv()
        total = prx[my_y, my_z]
        for slot in range(3):
            total = total + prc[slot].astype(F32)
        pgrad_ref[...] = total

    def tap_pair():
        return rep_copy(10, tap_own.at[sibling], tap_pair_in, 0, 0, 1)

    def tap_y(dy):
        return rep_copy(10 + dy, tap_own.at[core, (my_y + dy) & 3], tap_y_in.at[dy - 1], dy, 0, 0)

    def tap_z(dz, slot):
        return rep_copy(13 + dz, tap_z_all.at[my_z], tap_z_all.at[slot], 0, dz, 0)

    def tap_back_y(dy, slot):
        return rep_copy(16 + dy, tap_all.at[core, my_y], tap_all.at[core, slot], dy, 0, 0)

    def tap_back_pair(slot):
        return rep_copy(20, tap_all.at[core], tap_all.at[slot], 0, 0, 1)

    def taps_to_pair():
        sums = jnp.concatenate([jnp.sum(dka[...], axis=1), jnp.zeros((7, C), F32)], axis=0)
        for block in range(8):
            tap_own[block // 4, block & 3] = sums[:, block * LANES : block * LANES + LANES]
        tap_pair().start()

    def taps_to_y():
        tap_pair().wait_recv()
        tap_own[core] = tap_own[core] + tap_pair_in[...]
        for dy in (1, 2, 3):
            tap_y(dy).start()

    def taps_to_z():
        total = tap_own[core, my_y]
        for dy in (1, 2, 3):
            tap_y(dy).wait_recv()
            total = total + tap_y_in[dy - 1]
        tap_z_all[my_z] = total
        for dz in (1, 2, 3):
            tap_z(dz, my_z).start()

    def taps_back_y():
        for dz in (1, 2, 3):
            tap_z(dz, (my_z + 4 - dz) & 3).wait_recv()
        tap_all[core, my_y] = (tap_z_all[0] + tap_z_all[1]) + (tap_z_all[2] + tap_z_all[3])
        for dy in (1, 2, 3):
            tap_back_y(dy, my_y).start()

    def taps_back_pair():
        for dy in (1, 2, 3):
            tap_back_y(dy, (my_y + 4 - dy) & 3).wait_recv()
        tap_back_pair(core).start()

    def taps_end():
        tap_back_pair(sibling).wait_recv()
        sums = jnp.concatenate([tap_all[b // 4, b & 3] for b in range(8)], axis=1)
        for t in range(25):
            dgrad_ref[t] = sums[t : t + 1] * keep[t]

    loads[3].wait()
    forward(0)
    receive_g(0)
    backward(0)
    tap_grad(0)
    point_terms(0)
    forward(1)
    receive_g(1)
    point_terms(1)
    back_project(1)
    back_activate(1)
    point_over_y()
    convolve(1, gh32, -1, emit_gin)
    send_gin(1)
    seg_send(IM1, si.at[1], ri.at[1])
    send_last(fold_i, sil)
    seg_send(IL, sil, ril)
    tap_grad(1)
    taps_to_pair()
    point_over_z()
    taps_to_y()
    seg_wait(OM0, so.at[0], ro.at[0])
    seg_wait(OM1, so.at[1], ro.at[1])
    seg_wait(OL, sol, rol)
    taps_to_z()
    home(ro, rol, out_ref)
    store_out = pltpu.make_async_copy(out_ref, out_hbm, load_sem.at[4])
    store_out.start()
    taps_back_y()
    point_end()
    taps_back_pair()
    for j in range(2):
        seg_sent((XM0, XM1)[j], sx.at[j], rx.at[j])
        seg_sent((GM0, GM1)[j], sg.at[j], rg.at[j])
        seg_sent((OM0, OM1)[j], so.at[j], ro.at[j])
    seg_sent(IM0, si.at[0], ri.at[0])
    seg_sent(XL, sxl, rxl)
    seg_sent(GL, sgl, rgl)
    seg_sent(OL, sol, rol)
    for y in range(4):
        pair_copy(y).wait_send()
    tap_pair().wait_send()
    for d in (1, 2, 3):
        y_copy(d).wait_send()
        z_copy(d).wait_send()
        tap_y(d).wait_send()
        tap_z(d, my_z).wait_send()
    seg_wait(IM0, si.at[0], ri.at[0])
    seg_wait(IM1, si.at[1], ri.at[1])
    seg_wait(IL, sil, ril)
    home(ri, ril, gin_ref)
    store_gin = pltpu.make_async_copy(gin_ref, gin_hbm, load_sem.at[5])
    store_gin.start()
    taps_end()

    seg_sent(IM1, si.at[1], ri.at[1])
    seg_sent(IL, sil, ril)
    tap_back_pair(core).wait_send()
    for d in (1, 2, 3):
        tap_back_y(d, my_y).wait_send()
    store_out.wait()
    store_gin.wait()


def body(feature_maps, path_lists, point_weight, depth_kernel, cotangent):
    x = feature_maps.transpose(1, 2, 0, 3).reshape(POS * 8, C)
    g = cotangent.transpose(1, 2, 0, 3).reshape(POS * 8, C)
    vmem = pl.BlockSpec(memory_space=pltpu.VMEM)
    anywhere = pl.BlockSpec(memory_space=pl.ANY)
    maps = pltpu.VMEM((POS * 8, C), BF16)
    main = pltpu.VMEM((2, SEG, MAIN, C), BF16)
    last = pltpu.VMEM((SEG, 16, LANES), BF16)
    wide = pltpu.VMEM((2, ROWS, C), F32)
    narrow = pltpu.VMEM((2, ROWS, C), BF16)
    out, gin, pgrad, dgrad = pl.pallas_call(
        kernel,
        out_shape=(
            jax.ShapeDtypeStruct((POS * 8, C), BF16),
            jax.ShapeDtypeStruct((POS * 8, C), BF16),
            jax.ShapeDtypeStruct((32, C), F32),
            jax.ShapeDtypeStruct((25, 1, C), F32),
        ),
        in_specs=[pl.BlockSpec(memory_space=pltpu.SMEM)] + [anywhere] * 4,
        out_specs=[anywhere] * 2 + [vmem] * 2,
        scratch_shapes=[
            maps, maps, pltpu.VMEM((C, C), BF16), pltpu.VMEM((25, 1, C), F32), maps, maps,
            *[main, main, last, last] * 4,
            wide, wide, wide, wide, narrow, narrow,
            pltpu.VMEM((2, ROWS, LANES), F32),
            pltpu.VMEM((25, 8, C), F32),
            pltpu.VMEM((128, LANES), F32),
            pltpu.VMEM((128, LANES), F32),
            pltpu.VMEM((4, 4, 2, 32, C), F32),
            pltpu.VMEM((4, 4, 32, C), F32),
            pltpu.VMEM((3, 4, 32, C), BF16),
            pltpu.VMEM((3, 4, 32, C), BF16),
            pltpu.VMEM((3, 32, C), BF16),
            pltpu.VMEM((3, 32, C), BF16),
            pltpu.VMEM((25, 8, C), F32),
            pltpu.VMEM((2, 4, 32, LANES), F32),
            pltpu.VMEM((4, 32, LANES), F32),
            pltpu.VMEM((3, 32, LANES), F32),
            pltpu.VMEM((4, 32, LANES), F32),
            pltpu.VMEM((2, 4, 32, LANES), F32),
            pltpu.SemaphoreType.DMA((12, SEG)),
            pltpu.SemaphoreType.DMA((12, SEG)),
            pltpu.SemaphoreType.DMA((12,)),
            pltpu.SemaphoreType.DMA((21,)),
            pltpu.SemaphoreType.DMA((21,)),
            pltpu.SemaphoreType.DMA((6,)),
        ],
        compiler_params=pltpu.CompilerParams(
            collective_id=0, has_side_effects=True, vmem_limit_bytes=60 * 1024 * 1024
        ),
        name="supernet_window",
    )(path_lists[:, :, 0], x, g, point_weight[0, 0], depth_kernel[0].reshape(25, 1, C))
    final = out.reshape(SIDE, SIDE, 8, C).transpose(2, 0, 1, 3)
    grad = gin.reshape(SIDE, SIDE, 8, C).transpose(2, 0, 1, 3)
    return final, grad, pgrad[None, None], dgrad.reshape(1, 1, 25, C)


def solution(mesh):
    placed = (
        P(("segment", "rep"), None, None, None),
        P(None, ("segment", "rep"), None),
        P(None, "segment", None, None),
        P(None, "segment", None, None),
        P(("segment", "rep"), None, None, None),
    )
    return jax.shard_map(
        body,
        mesh=mesh,
        in_specs=placed,
        out_specs=(
            P(("segment", "rep"), None, None, None),
            P(("segment", "rep"), None, None, None),
            P(None, "segment", "rep", None),
            P(None, "segment", None, None),
        ),
        check_vma=False,
    )
```

```python
import functools

import jax
import jax.numpy as jnp
from jax import lax
from jax.experimental import pallas as pl
from jax.experimental.pallas import tpu as pltpu
from jax.sharding import PartitionSpec as P

MESH = pl.DeviceIdType.MESH
EPS = 1e-05
F32 = jnp.float32
BF16 = jnp.bfloat16

C = 1024
SIDE = 7
POS = SIDE * SIDE
MAIN = 48
ROWS = 400
LANES = 128
SEG = 8
PARTNERS = ((0, 2), (1, 2), (0, 1), (0, 3), (1, 1), (1, 3), (1, 0))

XM0, XM1, XL, GM0, GM1, GL, OM0, OM1, OL, IM0, IM1, IL = range(12)


def iota2(rows, cols):
    return (
        lax.broadcasted_iota(jnp.int32, (rows, cols), 0),
        lax.broadcasted_iota(jnp.int32, (rows, cols), 1),
    )


def onehot(cond):
    return jnp.where(cond, 1.0, 0.0)


def mm(a, b):
    return jnp.dot(a, b, preferred_element_type=F32)


def kernel(
    path_ref,
    x_in,
    g_in,
    w_in,
    k_in,
    out_hbm,
    gin_hbm,
    pgrad_ref,
    dgrad_ref,
    x_ref, g_ref, w_ref, k_ref, out_ref, gin_ref,
    sx, rx, sxl, rxl,
    sg, rg, sgl, rgl,
    so, ro, sol, rol,
    si, ri, sil, ril,
    x32, h32, gh32, g32, ab, gb, q128, kb,
    fold_o, fold_i,
    pg, prx, psb, prb, psc, prc,
    dka, tap_own, tap_pair_in, tap_y_in, tap_z_all, tap_all,
    send_sem, recv_sem, local_sem, rsend, rrecv, load_sem,
):
    me = lax.axis_index("segment")
    rep = lax.axis_index("rep")
    z_lo = me >> 2
    xx = me & 3
    my_y = rep >> 3
    my_z = (rep >> 1) & 3
    core = rep & 1

    def rep_at(dy, dz, dc):
        return (((my_y + dy) & 3) << 3) + (((my_z + dz) & 3) << 1) + ((core + dc) & 1)

    outside = rep_at(0, 2 * z_lo - 1, 0)

    def seg_at(dz, dx):
        return (((z_lo + dz) & 1) << 2) + ((xx + dx) & 3)

    def seg_device(dz, dx):
        return (seg_at(dz, dx), outside if dz and dx & 1 else rep)

    rep_partners = ((0, 0, 1), (1, 0, 0), (2, 0, 0), (3, 0, 0), (0, 1, 0), (0, 2, 0), (0, 3, 0))

    barrier = pltpu.get_barrier_semaphore()
    for dy, dz, dc in rep_partners:
        pl.semaphore_signal(
            barrier, inc=1, device_id=(me, rep_at(dy, dz, dc)), device_id_type=MESH
        )
    for dz, dx in PARTNERS:
        pl.semaphore_signal(barrier, inc=1, device_id=seg_device(dz, dx), device_id_type=MESH)

    loads = [
        pltpu.make_async_copy(far, near, load_sem.at[i])
        for i, (far, near) in enumerate(
            ((x_in, x_ref), (g_in, g_ref), (k_in, k_ref), (w_in, w_ref))
        )
    ]
    for load in loads:
        load.start()

    def seg_copy(kind, src, dst, dz, dx, received=False):
        there = seg_at(dz, dx)
        slot = there if received else me
        return pltpu.make_async_remote_copy(
            src_ref=src.at[there],
            dst_ref=dst.at[slot],
            send_sem=send_sem.at[kind, there],
            recv_sem=recv_sem.at[kind, slot],
            device_id=seg_device(dz, dx),
            device_id_type=MESH,
        )

    def seg_send(kind, src, dst):
        for dz, dx in PARTNERS:
            seg_copy(kind, src, dst, dz, dx).start()
        pltpu.make_async_copy(src.at[me], dst.at[me], local_sem.at[kind]).start()

    def seg_wait(kind, src, dst):
        pltpu.make_async_copy(src.at[me], dst.at[me], local_sem.at[kind]).wait()
        for dz, dx in PARTNERS:
            seg_copy(kind, src, dst, dz, dx, received=True).wait_recv()

    def seg_sent(kind, src, dst):
        for dz, dx in PARTNERS:
            seg_copy(kind, src, dst, dz, dx).wait_send()

    paths = [path_ref[0, i] for i in range(8)]
    slot_of = []
    for i in range(8):
        rank = jnp.int32(0)
        for earlier in range(i):
            rank = rank + jnp.where(paths[earlier] == paths[i], 1, 0)
        slot_of.append(2 * paths[i] + rank)

    def slots_like(sample):
        slots = jnp.full(sample.shape, -1, jnp.int32)
        for i in range(8):
            slots = jnp.where(sample == i, slot_of[i], slots)
        return slots

    m, n = iota2(256, 128)
    slots = slots_like(n & 7)
    wanted = 2 * ((m >> 4) & 7) + (m >> 7)
    route32 = onehot(((m & 15) == (n >> 3)) & (slots == wanted))
    route = route32.astype(BF16)
    route_back = route32.T.astype(BF16)
    m, n = iota2(128, 128)
    slots = slots_like(n & 7)
    route_last32 = onehot(((m & 7) == (n >> 3)) & (slots == (m >> 3)))
    route_last = route_last32.astype(BF16)
    route_last_back = route_last32.T.astype(BF16)
    to_rows = onehot(((m >> 3) == (n & 15)) & ((m & 7) == (n >> 4))).astype(BF16)
    from_rows = onehot(((m & 15) == (n >> 3)) & ((m >> 4) == (n & 7))).astype(BF16)
    unfold = onehot(
        ((m >> 4) == (n & 7)) & (((m >> 3) & 1) == ((n >> 3) & 1)) & ((m & 7) == (n >> 4))
    ).astype(BF16)
    refold = onehot(
        ((n >> 4) == (m & 7)) & (((n >> 3) & 1) == ((m >> 3) & 1)) & ((n & 7) == (m >> 4))
    ).astype(BF16)

    def dispatch(source, main, last):
        for q in range(3):
            for part in range(4):
                lanes = slice(part * 256, part * 256 + 256)
                moved = mm(route, source[q * 128 : q * 128 + 128, lanes]).astype(BF16)
                for j in range(2):
                    main[j, :, q * 16 : q * 16 + 16, lanes] = moved[
                        j * 128 : j * 128 + 128
                    ].reshape(8, 16, 256)
        tail = source[384:392, :].astype(F32)
        folded = jnp.concatenate(
            [tail[:, b * LANES : b * LANES + LANES] for b in range(8)]
            + [jnp.zeros((64, LANES), F32)],
            axis=0,
        ).astype(BF16)
        last[...] = mm(route_last, folded).astype(BF16).reshape(8, 16, LANES)

    loads[0].wait()
    dispatch(x_ref, sx, sxl)
    pl.semaphore_wait(barrier, 14)
    seg_send(XM0, sx.at[0], rx.at[0])
    seg_send(XL, sxl, rxl)
    loads[1].wait()
    dispatch(g_ref, sg, sgl)
    seg_send(GM0, sg.at[0], rg.at[0])
    seg_send(GL, sgl, rgl)
    seg_send(XM1, sx.at[1], rx.at[1])
    seg_send(GM1, sg.at[1], rg.at[1])

    loads[2].wait()
    kind = me % 3
    keep = []
    for t in range(25):
        row, col = t // 5 - 2, t % 5 - 2
        narrow = 1.0 if abs(row) <= 1 and abs(col) <= 1 else 0.0
        spaced = 1.0 if row % 2 == 0 and col % 2 == 0 else 0.0
        keep.append(jnp.where(kind == 0, narrow, jnp.where(kind == 1, 1.0, spaced)))
        kb[t] = jnp.broadcast_to(k_ref[t], (8, C)) * keep[t]
    dka[...] = jnp.zeros((25, 8, C), F32)
    for j in range(2):
        x32[j, 392:400, :] = jnp.zeros((8, C), F32)
        h32[j, 392:400, :] = jnp.zeros((8, C), F32)

    def receive_main(j, got, wide, narrow):
        for q in range(3):
            for part in range(4):
                lanes = slice(part * 256, part * 256 + 256)
                rows = mm(to_rows, got[j, :, q * 16 : q * 16 + 16, lanes].reshape(128, 256))
                wide[j, q * 128 : q * 128 + 128, lanes] = rows
                if narrow is not None:
                    narrow[j, q * 128 : q * 128 + 128, lanes] = rows.astype(BF16)

    def receive_last(got, wide, narrow):
        rows = mm(unfold, got[...].reshape(128, LANES))
        for j in range(2):
            row = jnp.concatenate(
                [rows[b * 16 + j * 8 : b * 16 + j * 8 + 8] for b in range(8)], axis=1
            )
            wide[j, 384:392, :] = row
            if narrow is not None:
                narrow[j, 384:400, :] = jnp.concatenate([row, jnp.zeros((8, C), F32)], 0).astype(BF16)

    def rows_at(ref, j, r, lanes):
        return [ref[j, (r * 7 + c) * 8 : (r * 7 + c) * 8 + 8, lanes] for c in range(7)]

    def convolve(j, source, sign, emit):
        def body(block, carry):
            lanes = pl.ds(pl.multiple_of(block * LANES, LANES), LANES)
            for r in range(7):
                acc = [None] * 7
                for dr in range(-2, 3):
                    at = r + sign * dr
                    if at < 0 or at > 6:
                        continue
                    row = rows_at(source, j, at, lanes)
                    for dc in range(-2, 3):
                        tap = kb[(dr + 2) * 5 + dc + 2, :, lanes]
                        for c in range(7):
                            ac = c + sign * dc
                            if ac < 0 or ac > 6:
                                continue
                            term = tap * row[ac]
                            acc[c] = term if acc[c] is None else acc[c] + term
                for c in range(7):
                    emit(j, (r * 7 + c) * 8, lanes, acc[c])
            return carry

        lax.fori_loop(0, 8, body, 0)

    def emit_h(j, row, lanes, value):
        h32[j, row : row + 8, lanes] = value

    def emit_gin(j, row, lanes, value):
        g32[j, row : row + 8, lanes] = g32[j, row : row + 8, lanes] + value

    def tap_grad(j):
        def body(block, carry):
            lanes = pl.ds(pl.multiple_of(block * LANES, LANES), LANES)
            for dr in range(-2, 3):
                acc = [None] * 5
                for r in range(7):
                    at = r + dr
                    if at < 0 or at > 6:
                        continue
                    grad = rows_at(gh32, j, r, lanes)
                    row = rows_at(x32, j, at, lanes)
                    for dc in range(-2, 3):
                        for c in range(7):
                            ac = c + dc
                            if ac < 0 or ac > 6:
                                continue
                            term = grad[c] * row[ac]
                            acc[dc + 2] = term if acc[dc + 2] is None else acc[dc + 2] + term
                for t in range(5):
                    at = (dr + 2) * 5 + t
                    dka[at, :, lanes] = dka[at, :, lanes] + acc[t]
            return carry

        lax.fori_loop(0, 8, body, 0)

    def activate(j):
        def body(step, carry):
            rows = pl.ds(pl.multiple_of(step * 80, 80), 80)
            h = h32[j, rows, :]
            q = lax.rsqrt(jnp.sum(h * h, axis=1, keepdims=True) * (1.0 / C) + EPS)
            z = h * q
            h32[j, rows, :] = z
            q128[j, rows, :] = jnp.broadcast_to(q, (80, LANES))
            ab[j, rows, :] = (z * jax.nn.sigmoid(z)).astype(BF16)
            return carry

        lax.fori_loop(0, 5, body, 0)

    def send_rows(j, value, n, main, fold):
        lanes = pl.ds(pl.multiple_of(n * 256, 256), 256)
        for q in range(3):
            moved = mm(from_rows, value[q * 128 : q * 128 + 128]).astype(BF16)
            main[j, :, q * 16 : q * 16 + 16, lanes] = moved.reshape(8, 16, 256)
        tail = value[384:400].astype(F32)
        for b in range(2):
            fold[pl.ds(pl.multiple_of((2 * n + b) * 16 + j * 8, 8), 8), :] = tail[
                :8, b * LANES : b * LANES + LANES
            ]

    def send_last(fold, last):
        last[...] = mm(refold, fold[...].astype(BF16)).astype(BF16).reshape(8, 16, LANES)

    def project(j):
        def body(n, carry):
            lanes = pl.ds(pl.multiple_of(n * 256, 256), 256)
            value = (x32[j, :, lanes] + mm(ab[j], w_ref[:, lanes])).astype(BF16)
            send_rows(j, value, n, so, fold_o)
            return carry

        lax.fori_loop(0, 4, body, 0)

    def back_project(j):
        def body(n, carry):
            lanes = pl.ds(pl.multiple_of(n * 256, 256), 256)
            gh32[j, :, lanes] = lax.dot_general(
                gb[j], w_ref[lanes, :], (((1,), (1,)), ((), ())), preferred_element_type=F32
            )
            return carry

        lax.fori_loop(0, 4, body, 0)

    def back_activate(j):
        def body(step, carry):
            rows = pl.ds(pl.multiple_of(step * 80, 80), 80)
            z = h32[j, rows, :]
            s = jax.nn.sigmoid(z)
            gz = gh32[j, rows, :] * s * (1.0 + z * (1.0 - s))
            mean = jnp.sum(gz * z, axis=1, keepdims=True) * (1.0 / C)
            q = jnp.concatenate([q128[j, rows, :]] * 8, axis=1)
            gh32[j, rows, :] = q * (gz - z * mean)
            return carry

        lax.fori_loop(0, 5, body, 0)

    def send_gin(j):
        def body(n, carry):
            lanes = pl.ds(pl.multiple_of(n * 256, 256), 256)
            send_rows(j, g32[j, :, lanes].astype(BF16), n, si, fold_i)
            return carry

        lax.fori_loop(0, 4, body, 0)

    def forward(j):
        seg_wait((XM0, XM1)[j], sx.at[j], rx.at[j])
        receive_main(j, rx, x32, None)
        if j == 0:
            seg_wait(XL, sxl, rxl)
            receive_last(rxl, x32, None)
        convolve(j, x32, 1, emit_h)
        activate(j)
        project(j)
        seg_send((OM0, OM1)[j], so.at[j], ro.at[j])
        if j == 1:
            send_last(fold_o, sol)
            seg_send(OL, sol, rol)

    def receive_g(j):
        seg_wait((GM0, GM1)[j], sg.at[j], rg.at[j])
        receive_main(j, rg, g32, gb)
        if j == 0:
            seg_wait(GL, sgl, rgl)
            receive_last(rgl, g32, gb)
            for i in range(2):
                g32[i, 392:400, :] = jnp.zeros((8, C), F32)

    def backward(j):
        back_project(j)
        back_activate(j)
        convolve(j, gh32, -1, emit_gin)
        send_gin(j)
        seg_send((IM0, IM1)[j], si.at[j], ri.at[j])

    def home(main, last, target):
        for q in range(3):
            for part in range(4):
                lanes = slice(part * 256, part * 256 + 256)
                got = jnp.concatenate(
                    [main[j, :, q * 16 : q * 16 + 16, lanes].reshape(128, 256) for j in range(2)],
                    axis=0,
                )
                target[q * 128 : q * 128 + 128, lanes] = mm(route_back, got).astype(BF16)
        rows = mm(route_last_back, last[...].reshape(128, LANES))
        target[384:392, :] = jnp.concatenate(
            [rows[b * 8 : b * 8 + 8] for b in range(8)], axis=1
        ).astype(BF16)

    def rep_copy(kind, src, dst, dy, dz, dc):
        return pltpu.make_async_remote_copy(
            src_ref=src,
            dst_ref=dst,
            send_sem=rsend.at[kind],
            recv_sem=rrecv.at[kind],
            device_id=(me, rep_at(dy, dz, dc)),
            device_id_type=MESH,
        )

    sibling = 1 - core

    def pair_copy(y):
        return rep_copy(y, pg.at[y, :, sibling], prx.at[y], 0, 0, 1)

    def point_terms(j):
        for dy in (1, 2, 3, 0):
            y = (my_y + dy) & 3
            cols = pl.ds(pl.multiple_of(y * 256, 256), 256)
            for part in range(4):
                lanes = slice(part * 256, part * 256 + 256)
                term = lax.dot_general(
                    ab[j, :, cols],
                    gb[j, :, lanes],
                    (((0,), (0,)), ((), ())),
                    preferred_element_type=F32,
                ).reshape(4, 2, 32, 256)
                if j == 0:
                    pg[y, :, :, :, lanes] = term
                else:
                    pg[y, :, :, :, lanes] = pg[y, :, :, :, lanes] + term
            if j == 1:
                pair_copy(y).start()

    def y_copy(dy):
        return rep_copy(3 + dy, psb.at[dy - 1], prb.at[dy - 1], dy, 0, 0)

    def z_copy(dz):
        return rep_copy(6 + dz, psc.at[dz - 1], prc.at[dz - 1], 0, dz, 0)

    def point_over_y():
        for dy in (1, 2, 3, 0):
            y = (my_y + dy) & 3
            pair_copy(y).wait_recv()
            total = pg[y, :, core] + prx[y]
            if dy:
                psb[dy - 1] = total.astype(BF16)
                y_copy(dy).start()
            else:
                prx[y] = total

    def point_over_z():
        total = prx[my_y]
        for dy in (1, 2, 3):
            y_copy(dy).wait_recv()
        for slot in range(3):
            total = total + prb[slot].astype(F32)
        prx[my_y] = total
        for dz in (1, 2, 3):
            psc[dz - 1] = prx[my_y, (my_z + dz) & 3].astype(BF16)
            z_copy(dz).start()

    def point_end():
        for dz in (1, 2, 3):
            z_copy(dz).wait_recv()
        total = prx[my_y, my_z]
        for slot in range(3):
            total = total + prc[slot].astype(F32)
        pgrad_ref[...] = total

    def tap_pair():
        return rep_copy(10, tap_own.at[sibling], tap_pair_in, 0, 0, 1)

    def tap_y(dy):
        return rep_copy(10 + dy, tap_own.at[core, (my_y + dy) & 3], tap_y_in.at[dy - 1], dy, 0, 0)

    def tap_z(dz, slot):
        return rep_copy(13 + dz, tap_z_all.at[my_z], tap_z_all.at[slot], 0, dz, 0)

    def tap_back_y(dy, slot):
        return rep_copy(16 + dy, tap_all.at[core, my_y], tap_all.at[core, slot], dy, 0, 0)

    def tap_back_pair(slot):
        return rep_copy(20, tap_all.at[core], tap_all.at[slot], 0, 0, 1)

    def taps_to_pair():
        sums = jnp.concatenate([jnp.sum(dka[...], axis=1), jnp.zeros((7, C), F32)], axis=0)
        for block in range(8):
            tap_own[block // 4, block & 3] = sums[:, block * LANES : block * LANES + LANES]
        tap_pair().start()

    def taps_to_y():
        tap_pair().wait_recv()
        tap_own[core] = tap_own[core] + tap_pair_in[...]
        for dy in (1, 2, 3):
            tap_y(dy).start()

    def taps_to_z():
        total = tap_own[core, my_y]
        for dy in (1, 2, 3):
            tap_y(dy).wait_recv()
            total = total + tap_y_in[dy - 1]
        tap_z_all[my_z] = total
        for dz in (1, 2, 3):
            tap_z(dz, my_z).start()

    def taps_back_y():
        for dz in (1, 2, 3):
            tap_z(dz, (my_z + 4 - dz) & 3).wait_recv()
        tap_all[core, my_y] = (tap_z_all[0] + tap_z_all[1]) + (tap_z_all[2] + tap_z_all[3])
        for dy in (1, 2, 3):
            tap_back_y(dy, my_y).start()

    def taps_back_pair():
        for dy in (1, 2, 3):
            tap_back_y(dy, (my_y + 4 - dy) & 3).wait_recv()
        tap_back_pair(core).start()

    def taps_end():
        tap_back_pair(sibling).wait_recv()
        sums = jnp.concatenate([tap_all[b // 4, b & 3] for b in range(8)], axis=1)
        for t in range(25):
            dgrad_ref[t] = sums[t : t + 1] * keep[t]

    loads[3].wait()
    forward(0)
    receive_g(0)
    backward(0)
    tap_grad(0)
    point_terms(0)
    forward(1)
    receive_g(1)
    point_terms(1)
    back_project(1)
    back_activate(1)
    convolve(1, gh32, -1, emit_gin)
    send_gin(1)
    point_over_y()
    seg_send(IM1, si.at[1], ri.at[1])
    send_last(fold_i, sil)
    seg_send(IL, sil, ril)
    tap_grad(1)
    taps_to_pair()
    point_over_z()
    taps_to_y()
    seg_wait(OM0, so.at[0], ro.at[0])
    seg_wait(OM1, so.at[1], ro.at[1])
    seg_wait(OL, sol, rol)
    taps_to_z()
    home(ro, rol, out_ref)
    store_out = pltpu.make_async_copy(out_ref, out_hbm, load_sem.at[4])
    store_out.start()
    taps_back_y()
    point_end()
    taps_back_pair()
    for j in range(2):
        seg_sent((XM0, XM1)[j], sx.at[j], rx.at[j])
        seg_sent((GM0, GM1)[j], sg.at[j], rg.at[j])
        seg_sent((OM0, OM1)[j], so.at[j], ro.at[j])
    seg_sent(IM0, si.at[0], ri.at[0])
    seg_sent(XL, sxl, rxl)
    seg_sent(GL, sgl, rgl)
    seg_sent(OL, sol, rol)
    for y in range(4):
        pair_copy(y).wait_send()
    tap_pair().wait_send()
    for d in (1, 2, 3):
        y_copy(d).wait_send()
        z_copy(d).wait_send()
        tap_y(d).wait_send()
        tap_z(d, my_z).wait_send()
    seg_wait(IM0, si.at[0], ri.at[0])
    seg_wait(IM1, si.at[1], ri.at[1])
    seg_wait(IL, sil, ril)
    home(ri, ril, gin_ref)
    store_gin = pltpu.make_async_copy(gin_ref, gin_hbm, load_sem.at[5])
    store_gin.start()
    taps_end()

    seg_sent(IM1, si.at[1], ri.at[1])
    seg_sent(IL, sil, ril)
    tap_back_pair(core).wait_send()
    for d in (1, 2, 3):
        tap_back_y(d, my_y).wait_send()
    store_out.wait()
    store_gin.wait()


def body(feature_maps, path_lists, point_weight, depth_kernel, cotangent):
    x = feature_maps.transpose(1, 2, 0, 3).reshape(POS * 8, C)
    g = cotangent.transpose(1, 2, 0, 3).reshape(POS * 8, C)
    vmem = pl.BlockSpec(memory_space=pltpu.VMEM)
    anywhere = pl.BlockSpec(memory_space=pl.ANY)
    maps = pltpu.VMEM((POS * 8, C), BF16)
    main = pltpu.VMEM((2, SEG, MAIN, C), BF16)
    last = pltpu.VMEM((SEG, 16, LANES), BF16)
    wide = pltpu.VMEM((2, ROWS, C), F32)
    narrow = pltpu.VMEM((2, ROWS, C), BF16)
    out, gin, pgrad, dgrad = pl.pallas_call(
        kernel,
        out_shape=(
            jax.ShapeDtypeStruct((POS * 8, C), BF16),
            jax.ShapeDtypeStruct((POS * 8, C), BF16),
            jax.ShapeDtypeStruct((32, C), F32),
            jax.ShapeDtypeStruct((25, 1, C), F32),
        ),
        in_specs=[pl.BlockSpec(memory_space=pltpu.SMEM)] + [anywhere] * 4,
        out_specs=[anywhere] * 2 + [vmem] * 2,
        scratch_shapes=[
            maps, maps, pltpu.VMEM((C, C), BF16), pltpu.VMEM((25, 1, C), F32), maps, maps,
            *[main, main, last, last] * 4,
            wide, wide, wide, wide, narrow, narrow,
            pltpu.VMEM((2, ROWS, LANES), F32),
            pltpu.VMEM((25, 8, C), F32),
            pltpu.VMEM((128, LANES), F32),
            pltpu.VMEM((128, LANES), F32),
            pltpu.VMEM((4, 4, 2, 32, C), F32),
            pltpu.VMEM((4, 4, 32, C), F32),
            pltpu.VMEM((3, 4, 32, C), BF16),
            pltpu.VMEM((3, 4, 32, C), BF16),
            pltpu.VMEM((3, 32, C), BF16),
            pltpu.VMEM((3, 32, C), BF16),
            pltpu.VMEM((25, 8, C), F32),
            pltpu.VMEM((2, 4, 32, LANES), F32),
            pltpu.VMEM((4, 32, LANES), F32),
            pltpu.VMEM((3, 32, LANES), F32),
            pltpu.VMEM((4, 32, LANES), F32),
            pltpu.VMEM((2, 4, 32, LANES), F32),
            pltpu.SemaphoreType.DMA((12, SEG)),
            pltpu.SemaphoreType.DMA((12, SEG)),
            pltpu.SemaphoreType.DMA((12,)),
            pltpu.SemaphoreType.DMA((21,)),
            pltpu.SemaphoreType.DMA((21,)),
            pltpu.SemaphoreType.DMA((6,)),
        ],
        compiler_params=pltpu.CompilerParams(
            collective_id=0, has_side_effects=True, vmem_limit_bytes=60 * 1024 * 1024
        ),
        name="supernet_window",
    )(path_lists[:, :, 0], x, g, point_weight[0, 0], depth_kernel[0].reshape(25, 1, C))
    final = out.reshape(SIDE, SIDE, 8, C).transpose(2, 0, 1, 3)
    grad = gin.reshape(SIDE, SIDE, 8, C).transpose(2, 0, 1, 3)
    return final, grad, pgrad[None, None], dgrad.reshape(1, 1, 25, C)


def solution(mesh):
    placed = (
        P(("segment", "rep"), None, None, None),
        P(None, ("segment", "rep"), None),
        P(None, "segment", None, None),
        P(None, "segment", None, None),
        P(("segment", "rep"), None, None, None),
    )
    return jax.shard_map(
        body,
        mesh=mesh,
        in_specs=placed,
        out_specs=(
            P(("segment", "rep"), None, None, None),
            P(("segment", "rep"), None, None, None),
            P(None, "segment", "rep", None),
            P(None, "segment", None, None),
        ),
        check_vma=False,
    )
```
